256 devices in a mesh: row: 32 (over z_hi, x, core), col: 8 (over z_lo, y).
Axes of the slice: x: 4, y: 4, z: 8 (z_hi: 4, z_lo: 2; z = z_hi * 2 + z_lo), core: 2. Of those that a mesh axis runs over, the one named last changes fastest.
Arguments:
- eta_ladder: bfloat16 [20480, 1024], P('row', 'col'), may hold values from -1.0546875 to 1.0546875
- gamma_ladder: bfloat16 [20480, 1024], P('row', 'col'), may hold values from -1.0546875 to 1.0546875
- occupation: int32 [1024], replicated, may hold values from 0 to 4
- gamma: bfloat16 [20480, 20480], P('row', 'col'), may hold values from -6 to 6
Outputs:
- gamma_next: bfloat16 [20480, 20480], P('row', 'col')
The draws below stay inside these ranges and needn't reach their ends.
All inputs are finite; a program needn't handle non-finite values.
Results may differ from the reference program's by a relative error of at most 0.001.
Values may be sent and summed in bfloat16 or wider, within the bound.
No kernel may reach another device: no remote copies, remote signals or barrier semaphores. Data moves between devices by JAX's collectives and lax.ppermute only.
A program may use at most 128 MiB of HBM per device.

```python
import jax
import jax.numpy as jnp
from jax import lax

N = 20480
K = 1024
N_ROW = 32


def touch_ends(entries, key, least, high):
    index_at = [jax.random.randint(jax.random.fold_in(key, axis), (), 0, length) for axis, length in enumerate(entries.shape)]
    longest = entries.shape.index(max(entries.shape))
    neighbour = index_at[:longest] + [(index_at[longest] + 1) % entries.shape[longest]] + index_at[longest + 1:]
    return entries.at[tuple(index_at)].set(least).at[tuple(neighbour)].set(high)


def shard_levels(stream_key, dims, shards, least, top_value):
    gain, own = 1.0, jax.random.fold_in(stream_key, 6)
    for dim, parts in shards:
        draws = jnp.exp(jax.random.uniform(jax.random.fold_in(own, dim), (parts,), jnp.float32, least / len(shards), top_value / len(shards)))
        gain = gain * jnp.repeat(draws, dims[dim] // parts).reshape([-1 if axis == dim else 1 for axis in range(len(dims))])
    return gain


def noise(stream_key, shape, deviation, limit, pieces=(), kind=jnp.bfloat16):
    result = jax.random.normal(stream_key, shape, jnp.float32) * deviation
    if len(pieces) > 0:
        result = shard_levels(stream_key, shape, pieces, -0.22, 0.18) * result
    return jnp.clip(result, min=-limit, max=limit).astype(kind)


def setup_inputs(seed: int = 0) -> dict:
    splits = jax.random.split(jax.random.key(seed), 5)
    return {
        "eta_ladder": noise(splits[0], (N, K), (1.0 / K ** 0.25), 1.0546875, ((0, 32), (1, 8))),
        "gamma_ladder": noise(splits[1], (N, K), (1.0 / K ** 0.25), 1.0546875, ((0, 32), (1, 8))),
        "occupation": touch_ends(jax.random.randint(splits[2], (K,), 0, 5), jax.random.fold_in(splits[2], 1), 0, 4).astype(jnp.int32),
        "gamma": noise(splits[3], (N, N), 1.0, 6.0, ((0, 32), (1, 8))),
    }


euler_step = 0.5


def reference(eta_ladder, gamma_ladder, occupation, gamma):
    weights = 1.0 - 0.5 * occupation.astype(jnp.float32)
    left_panel = jnp.concatenate([(eta_ladder.astype(jnp.float32) * weights).astype(jnp.bfloat16), (gamma_ladder.astype(jnp.float32) * weights).astype(jnp.bfloat16)], 1)
    right_panel = jnp.concatenate([gamma_ladder, eta_ladder], 1)
    height = N // N_ROW
    left_blocks = left_panel.reshape(N_ROW, height, 2 * K)
    gamma_blocks = gamma.reshape(N_ROW, height, N)

    def one_block(pair):
        block_left, block_gamma = pair
        commutator = lax.dot_general(block_left, right_panel, (((1,), (1,)), ((), ())), preferred_element_type=jnp.float32)
        return (block_gamma.astype(jnp.float32) + euler_step * commutator).astype(jnp.bfloat16)

    return lax.map(one_block, (left_blocks, gamma_blocks)).reshape(N, N)
```

```python
import functools

import jax
import jax.numpy as jnp
from jax import lax
from jax.experimental import pallas as pl
from jax.experimental.pallas import tpu as pltpu
from jax.sharding import PartitionSpec as P

euler_step = 0.5
ZH, X, CORE, ZL, Y = 4, 4, 2, 2, 4
AXES = ("row", "col")


def every_device():
    for zh in range(ZH):
        for x in range(X):
            for core in range(CORE):
                for zl in range(ZL):
                    for y in range(Y):
                        yield zh, x, core, zl, y


def flat(zh, x, core, zl, y):
    return ((((zh % ZH) * X + x % X) * CORE + core % CORE) * ZL + zl % ZL) * Y + y % Y


def home(zh, x, core, zl, y):
    group = zh * 2 + x // 2
    return flat(zh + 2 * core + x % 2, y + 2 * core, zl, group // Y, group % Y)


def pairs(target):
    return [(flat(*d), target(*d)) for d in every_device()]


TO_HOME = pairs(home)
ALONG_Z = pairs(lambda zh, x, core, zl, y: flat(zh + 1 - 2 * core, x, core, zl, y))
ALONG_X = pairs(lambda zh, x, core, zl, y: flat(zh, x + 1 - 2 * core, core, zl, y))
OTHER_CORE = pairs(lambda zh, x, core, zl, y: flat(zh, x, core + 1, zl, y))


def send(value, way):
    return lax.ppermute(value, AXES, way)


def other(value):
    return send(value, OTHER_CORE)


def after(value, *earlier):
    return lax.optimization_barrier((value, *earlier))[0]


def weigh(panel_ref, weights_ref, out_ref):
    half = panel_ref.shape[-1] // 2
    weights = weights_ref[...]
    panel = panel_ref[...].astype(jnp.float32)
    out_ref[:, :half] = (panel[:, half:] * weights).astype(jnp.bfloat16)
    out_ref[:, half:] = (panel[:, :half] * weights).astype(jnp.bfloat16)


def left_panel_of(gathered, weights):
    parts, height, width = gathered.shape
    return pl.pallas_call(
        weigh,
        grid=(parts,),
        in_specs=[
            pl.BlockSpec((None, height, width), lambda k: (k, 0, 0)),
            pl.BlockSpec((None, 1, width // 2), lambda k: (k, 0, 0)),
        ],
        out_specs=pl.BlockSpec((height, width), lambda k: (0, k)),
        out_shape=jax.ShapeDtypeStruct((height, parts * width), jnp.bfloat16),
        compiler_params=pltpu.CompilerParams(vmem_limit_bytes=8 * 2**20),
        cost_estimate=pl.CostEstimate(
            flops=parts * height * width, bytes_accessed=4 * parts * height * width, transcendentals=0
        ),
        name="weigh_left",
    )(gathered, weights.reshape(parts, 1, width // 2))


def rem(value, length):
    return lax.rem(value, jnp.int32(length))


def block_kernel(dz, places, left_ref, *refs):
    count = len(places)
    pieces, gamma_ref = refs[:count], refs[count]
    out_ref, right, old, new, sems = refs[-5:]
    height, width = pieces[0].shape
    row, col = lax.axis_index("row"), lax.axis_index("col")
    zh, x, core = lax.div(row, jnp.int32(X * CORE)), rem(lax.div(row, jnp.int32(CORE)), X), rem(row, CORE)
    way = 2 * core - 1
    turn = rem(zh + dz[0] + dz[1] * way + 2 * ZH - lax.div(col, jnp.int32(2)), ZH)
    low, high = rem(turn, 2), lax.div(turn, jnp.int32(2))
    columns = pl.ds(pl.multiple_of((low * 2 + high) * height, 128), height)
    copies = [pltpu.make_async_copy(gamma_ref.at[:, columns], old, sems.at[count])]
    for index, (piece, (dx, other_core)) in enumerate(zip(pieces, places)):
        part = rem(core + other_core, CORE) * Y + rem(x + dx[0] + dx[1] * way + 2 * X - 2 * high, X)
        place = pl.ds(pl.multiple_of(part * width, width), width)
        copies.append(pltpu.make_async_copy(piece, right.at[:, place], sems.at[index]))
    for copy in copies:
        copy.start()
    for copy in copies:
        copy.wait()
    for first in range(0, height, 256):
        size = min(256, height - first)
        commutator = lax.dot_general(
            left_ref[...],
            right[first : first + size, :],
            (((1,), (1,)), ((), ())),
            preferred_element_type=jnp.float32,
        )
        new[:, first : first + size] = (
            old[:, first : first + size].astype(jnp.float32) + euler_step * commutator
        ).astype(jnp.bfloat16)
    back = pltpu.make_async_copy(new, out_ref.at[:, columns], sems.at[count + 1])
    back.start()
    back.wait()


def block_step(dz, places, left, pieces, gamma, out):
    count = len(pieces)
    height, width = pieces[0].shape
    anywhere = pl.BlockSpec(memory_space=pl.ANY)
    operands = [left, *pieces, gamma]
    aliases = {}
    if out is not None:
        aliases = {len(operands): 0}
        operands.append(out)
    return pl.pallas_call(
        functools.partial(block_kernel, dz, places),
        in_specs=[
            pl.BlockSpec(memory_space=pltpu.VMEM),
            *[anywhere] * (len(operands) - 1),
        ],
        out_specs=anywhere,
        out_shape=jax.ShapeDtypeStruct(gamma.shape, gamma.dtype),
        input_output_aliases=aliases,
        scratch_shapes=[
            pltpu.VMEM((height, count * width), jnp.bfloat16),
            pltpu.VMEM((height, height), jnp.bfloat16),
            pltpu.VMEM((height, height), jnp.bfloat16),
            pltpu.SemaphoreType.DMA((count + 2,)),
        ],
        compiler_params=pltpu.CompilerParams(vmem_limit_bytes=20 * 2**20),
        cost_estimate=pl.CostEstimate(
            flops=2 * height * height * count * width,
            bytes_accessed=4 * height * count * width + 4 * height * height,
            transcendentals=0,
        ),
        name="block_step",
    )(*operands)


HERE, BACK, AHEAD, ACROSS = (0, 0), (0, 1), (0, -1), (2, 0)
ALIKE = [(HERE, 0), (HERE, 1), (BACK, 0), (BACK, 1), (AHEAD, 1), (AHEAD, 0), (ACROSS, 0), (ACROSS, 1)]
DIRECT = [(HERE, 0), (HERE, 1), (BACK, 0), (BACK, 1), (AHEAD, 0), (AHEAD, 1), (ACROSS, 0), (ACROSS, 1)]
SWAPPED = [(dx, 1 - core) for dx, core in DIRECT]


def per_device(eta_ladder, gamma_ladder, occupation, gamma):
    weights = 1.0 - 0.5 * occupation.astype(jnp.float32)
    shard = jnp.concatenate([gamma_ladder, eta_ladder], 1)
    gathered = lax.all_gather(shard, "col")
    left = left_panel_of(gathered, weights)

    p = send(shard, TO_HOME)
    ps = other(p)
    za, zb = send(p, ALONG_Z), send(ps, ALONG_Z)
    xp, xps = send(p, ALONG_X), send(ps, ALONG_X)
    fxp = send(xp, ALONG_X)
    z2 = send(za, ALONG_Z)
    sa, sb = other(za), other(zb)
    z2s = other(z2)
    xza, xzb = send(za, ALONG_X), send(zb, ALONG_X)
    xsa, xsb = send(sa, ALONG_X), send(sb, ALONG_X)
    fxza, fxzb = send(xza, ALONG_X), send(xzb, ALONG_X)
    xz2, xz2s = send(z2, ALONG_X), send(z2s, ALONG_X)
    block0 = [p, ps, xp, xps, other(xp), other(xps), fxp, other(fxp)]
    out = block_step(HERE, ALIKE, left, block0, gamma, None)
    fxz2 = send(after(xz2, out), ALONG_X)
    blocka = [za, zb, xza, xzb, other(xsa), other(xsb), fxza, fxzb]
    blockb = [sa, sb, xsa, xsb, other(xza), other(xzb), other(fxza), other(fxzb)]
    block2 = [z2, z2s, xz2, xz2s, other(xz2), other(xz2s), fxz2, other(fxz2)]
    out = block_step(BACK, DIRECT, left, blocka, gamma, out)
    out = block_step(AHEAD, SWAPPED, left, blockb, gamma, out)
    return block_step(ACROSS, ALIKE, left, block2, gamma, out)


def solution(mesh):
    placed = (P("row", "col"), P("row", "col"), P(), P("row", "col"))
    return jax.shard_map(
        per_device, mesh=mesh, in_specs=placed, out_specs=P("row", "col"), check_vma=False
    )
```

```python
import functools

import jax
import jax.numpy as jnp
from jax import lax
from jax.experimental import pallas as pl
from jax.experimental.pallas import tpu as pltpu
from jax.sharding import PartitionSpec as P

euler_step = 0.5
ZH, X, CORE, ZL, Y = 4, 4, 2, 2, 4
AXES = ("row", "col")


def every_device():
    for zh in range(ZH):
        for x in range(X):
            for core in range(CORE):
                for zl in range(ZL):
                    for y in range(Y):
                        yield zh, x, core, zl, y


def flat(zh, x, core, zl, y):
    return ((((zh % ZH) * X + x % X) * CORE + core % CORE) * ZL + zl % ZL) * Y + y % Y


def home(zh, x, core, zl, y):
    group = zh * 2 + x // 2
    return flat(zh + 2 * core + x % 2, y + 2 * core, zl, group // Y, group % Y)


def pairs(target):
    return [(flat(*d), target(*d)) for d in every_device()]


TO_HOME = pairs(home)
ALONG_Z = pairs(lambda zh, x, core, zl, y: flat(zh + 1 - 2 * core, x, core, zl, y))
ALONG_X = pairs(lambda zh, x, core, zl, y: flat(zh, x + 1 - 2 * core, core, zl, y))
OTHER_CORE = pairs(lambda zh, x, core, zl, y: flat(zh, x, core + 1, zl, y))


def send(value, way):
    return lax.ppermute(value, AXES, way)


def other(value):
    return send(value, OTHER_CORE)


def after(value, *earlier):
    return lax.optimization_barrier((value, *earlier))[0]


def weigh(panel_ref, weights_ref, out_ref):
    half = panel_ref.shape[-1] // 2
    weights = weights_ref[...]
    panel = panel_ref[...].astype(jnp.float32)
    out_ref[:, :half] = (panel[:, half:] * weights).astype(jnp.bfloat16)
    out_ref[:, half:] = (panel[:, :half] * weights).astype(jnp.bfloat16)


def left_panel_of(gathered, weights):
    parts, height, width = gathered.shape
    return pl.pallas_call(
        weigh,
        grid=(parts,),
        in_specs=[
            pl.BlockSpec((None, height, width), lambda k: (k, 0, 0)),
            pl.BlockSpec((None, 1, width // 2), lambda k: (k, 0, 0)),
        ],
        out_specs=pl.BlockSpec((height, width), lambda k: (0, k)),
        out_shape=jax.ShapeDtypeStruct((height, parts * width), jnp.bfloat16),
        compiler_params=pltpu.CompilerParams(vmem_limit_bytes=8 * 2**20),
        cost_estimate=pl.CostEstimate(
            flops=parts * height * width, bytes_accessed=4 * parts * height * width, transcendentals=0
        ),
        name="weigh_left",
    )(gathered, weights.reshape(parts, 1, width // 2))


def rem(value, length):
    return lax.rem(value, jnp.int32(length))


def join(left_ref, right_ref, out_ref):
    half = left_ref.shape[-1]
    out_ref[:, :half] = left_ref[...]
    out_ref[:, half:] = right_ref[...]


def side_by_side(first, second):
    height, width = first.shape
    return pl.pallas_call(
        join,
        out_shape=jax.ShapeDtypeStruct((height, 2 * width), first.dtype),
        compiler_params=pltpu.CompilerParams(vmem_limit_bytes=4 * 2**20),
        name="join_shard",
    )(first, second)


def block_kernel(dz, places, operands, height, left_ref, *refs):
    arrays, gamma_ref = refs[:operands], refs[operands]
    out_ref, right, old, new, sems = refs[-5:]
    width = arrays[0].shape[-1]
    row, col = lax.axis_index("row"), lax.axis_index("col")
    zh, x, core = lax.div(row, jnp.int32(X * CORE)), rem(lax.div(row, jnp.int32(CORE)), X), rem(row, CORE)
    way = 2 * core - 1
    turn = rem(zh + dz[0] + dz[1] * way + 2 * ZH - lax.div(col, jnp.int32(2)), ZH)
    low, high = rem(turn, 2), lax.div(turn, jnp.int32(2))
    start = (low * 2 + high) * height
    spots = []
    for dx, other_core in (place[2:] for place in places):
        part = rem(core + other_core, CORE) * Y + rem(x + dx[0] + dx[1] * way + 2 * X - 2 * high, X)
        spots.append(pl.ds(pl.multiple_of(part * width, width), width))
    chunks = [(first, min(256, height - first)) for first in range(0, height, 256)]
    coming = []
    for turn_of, (first, size) in enumerate(chunks):
        columns = pl.ds(pl.multiple_of(start + first, 128), size)
        copies = [pltpu.make_async_copy(gamma_ref.at[:, columns], old.at[:, pl.ds(first, size)], sems.at[turn_of, 0])]
        for index, ((array, skip, _, _), spot) in enumerate(zip(places, spots)):
            copies.append(
                pltpu.make_async_copy(
                    arrays[array].at[pl.ds(skip * height + first, size), :],
                    right.at[pl.ds(first, size), spot],
                    sems.at[turn_of, 1 + index],
                )
            )
        for copy in copies:
            copy.start()
        coming.append(copies)
    going = []
    for turn_of, (first, size) in enumerate(chunks):
        for copy in coming[turn_of]:
            copy.wait()
        commutator = lax.dot_general(
            left_ref[...],
            right[first : first + size, :],
            (((1,), (1,)), ((), ())),
            preferred_element_type=jnp.float32,
        )
        new[:, first : first + size] = (
            old[:, first : first + size].astype(jnp.float32) + euler_step * commutator
        ).astype(jnp.bfloat16)
        columns = pl.ds(pl.multiple_of(start + first, 128), size)
        copy = pltpu.make_async_copy(new.at[:, pl.ds(first, size)], out_ref.at[:, columns], sems.at[turn_of, 1 + len(places)])
        copy.start()
        going.append(copy)
    for copy in going:
        copy.wait()


def block_step(dz, pieces, left, gamma, out):
    arrays = []
    places = []
    for array, skip, dx, core in pieces:
        known = [index for index, had in enumerate(arrays) if had is array]
        if not known:
            known = [len(arrays)]
            arrays.append(array)
        places.append((known[0], skip, dx, core))
    height, count, width = left.shape[0], len(pieces), arrays[0].shape[-1]
    anywhere = pl.BlockSpec(memory_space=pl.ANY)
    operands = [left, *arrays, gamma]
    aliases = {}
    if out is not None:
        aliases = {len(operands): 0}
        operands.append(out)
    return pl.pallas_call(
        functools.partial(block_kernel, dz, places, len(arrays), height),
        in_specs=[
            pl.BlockSpec(memory_space=pltpu.VMEM),
            *[anywhere] * (len(operands) - 1),
        ],
        out_specs=anywhere,
        out_shape=jax.ShapeDtypeStruct(gamma.shape, gamma.dtype),
        input_output_aliases=aliases,
        scratch_shapes=[
            pltpu.VMEM((height, count * width), jnp.bfloat16),
            pltpu.VMEM((height, height), jnp.bfloat16),
            pltpu.VMEM((height, height), jnp.bfloat16),
            pltpu.SemaphoreType.DMA((3, count + 2)),
        ],
        compiler_params=pltpu.CompilerParams(vmem_limit_bytes=20 * 2**20),
        cost_estimate=pl.CostEstimate(
            flops=2 * height * height * count * width,
            bytes_accessed=4 * height * count * width + 4 * height * height,
            transcendentals=0,
        ),
        name="block_step",
    )(*operands)


HERE, BACK, AHEAD, ACROSS = (0, 0), (0, 1), (0, -1), (2, 0)


def per_device(eta_ladder, gamma_ladder, occupation, gamma):
    weights = 1.0 - 0.5 * occupation.astype(jnp.float32)
    shard = side_by_side(gamma_ladder, eta_ladder)
    gathered = lax.all_gather(shard, "col")
    left = left_panel_of(gathered, weights)
    height = shard.shape[0]

    p = send(shard, TO_HOME)
    ps = other(p)
    xp, xps = send(p, ALONG_X), send(ps, ALONG_X)
    zz = send(jnp.concatenate([p, ps], 0), ALONG_Z)
    fxp = send(xp, ALONG_X)
    zz = after(zz, xps, fxp)
    zs = other(zz)
    z2 = send(zz[:height], ALONG_Z)
    z2s = other(z2)
    xzz, xzs = send(zz, ALONG_X), send(zs, ALONG_X)
    fxzz = send(xzz, ALONG_X)
    xz2, xz2s = send(z2, ALONG_X), send(z2s, ALONG_X)

    def alike(mine, swapped, x_mine, x_swapped, fx_mine):
        return [
            (mine, 0, HERE, 0),
            (swapped, 0, HERE, 1),
            (x_mine, 0, BACK, 0),
            (x_swapped, 0, BACK, 1),
            (other(x_mine), 0, AHEAD, 1),
            (other(x_swapped), 0, AHEAD, 0),
            (fx_mine, 0, ACROSS, 0),
            (other(fx_mine), 0, ACROSS, 1),
        ]

    def both(arrays, first_core):
        return [
            (array, half, dx, core)
            for array, dx in zip(arrays, (HERE, BACK, AHEAD, ACROSS))
            for half, core in ((0, first_core), (1, 1 - first_core))
        ]

    out = block_step(HERE, alike(p, ps, xp, xps, fxp), left, gamma, None)
    out = block_step(BACK, both([zz, xzz, other(xzs), fxzz], 0), left, gamma, out)
    fxz2 = send(after(xz2, out), ALONG_X)
    out = block_step(AHEAD, both([zs, xzs, other(xzz), other(fxzz)], 1), left, gamma, out)
    return block_step(ACROSS, alike(z2, z2s, xz2, xz2s, fxz2), left, gamma, out)


def solution(mesh):
    placed = (P("row", "col"), P("row", "col"), P(), P("row", "col"))
    return jax.shard_map(
        per_device, mesh=mesh, in_specs=placed, out_specs=P("row", "col"), check_vma=False
    )
```

```python
import functools

import jax
import jax.numpy as jnp
from jax import lax
from jax.experimental import pallas as pl
from jax.experimental.pallas import tpu as pltpu
from jax.sharding import PartitionSpec as P

euler_step = 0.5
ZH, X, CORE, ZL, Y = 4, 4, 2, 2, 4
AXES = ("row", "col")


def every_device():
    for zh in range(ZH):
        for x in range(X):
            for core in range(CORE):
                for zl in range(ZL):
                    for y in range(Y):
                        yield zh, x, core, zl, y


def flat(zh, x, core, zl, y):
    return ((((zh % ZH) * X + x % X) * CORE + core % CORE) * ZL + zl % ZL) * Y + y % Y


def home(zh, x, core, zl, y):
    group = zh * 2 + x // 2
    return flat(zh + 2 * core + x % 2, y + 2 * core, zl, group // Y, group % Y)


def pairs(target):
    return [(flat(*d), target(*d)) for d in every_device()]


TO_HOME = pairs(home)
ALONG_Z = pairs(lambda zh, x, core, zl, y: flat(zh + 1 - 2 * core, x, core, zl, y))
ALONG_X = pairs(lambda zh, x, core, zl, y: flat(zh, x + 1 - 2 * core, core, zl, y))
OTHER_ZL = pairs(lambda zh, x, core, zl, y: flat(zh, x, core, zl + 1, y))
OTHER_CORE = pairs(lambda zh, x, core, zl, y: flat(zh, x, core + 1, zl, y))


def send(value, way):
    return lax.ppermute(value, AXES, way)


def other(value):
    return send(value, OTHER_CORE)


def after(value, *earlier):
    return lax.optimization_barrier((value, *earlier))[0]


def weigh(panel_ref, weights_ref, out_ref):
    half = panel_ref.shape[-1] // 2
    k = pl.program_id(0)
    side = rem(lax.div(lax.axis_index("col"), jnp.int32(Y)) + k, ZL)
    weights = weights_ref[side * Y + lax.div(k, jnp.int32(ZL))]
    panel = panel_ref[...].astype(jnp.float32)
    out_ref[:, :half] = (panel[:, half:] * weights).astype(jnp.bfloat16)
    out_ref[:, half:] = (panel[:, :half] * weights).astype(jnp.bfloat16)


def left_panel_of(gathered, weights):
    parts, height, width = gathered.shape
    return pl.pallas_call(
        weigh,
        grid=(parts,),
        in_specs=[
            pl.BlockSpec((None, height, width), lambda k: (k, 0, 0)),
            pl.BlockSpec((parts, 1, width // 2), lambda k: (0, 0, 0)),
        ],
        out_specs=pl.BlockSpec((None, height, width), lambda k: (k, 0, 0)),
        out_shape=jax.ShapeDtypeStruct((parts, height, width), jnp.bfloat16),
        compiler_params=pltpu.CompilerParams(vmem_limit_bytes=8 * 2**20),
        cost_estimate=pl.CostEstimate(
            flops=parts * height * width, bytes_accessed=4 * parts * height * width, transcendentals=0
        ),
        name="weigh_left",
    )(gathered, weights.reshape(parts, 1, width // 2))


def rem(value, length):
    return lax.rem(value, jnp.int32(length))


def join(left_ref, right_ref, out_ref):
    half = left_ref.shape[-1]
    out_ref[:, :half] = left_ref[...]
    out_ref[:, half:] = right_ref[...]


def side_by_side(first, second):
    height, width = first.shape
    return pl.pallas_call(
        join,
        out_shape=jax.ShapeDtypeStruct((height, 2 * width), first.dtype),
        compiler_params=pltpu.CompilerParams(vmem_limit_bytes=4 * 2**20),
        name="join_shard",
    )(first, second)


def block_kernel(dz, places, operands, height, left_ref, *refs):
    arrays, gamma_ref = refs[:operands], refs[operands]
    out_ref, old, new, sems = refs[-4:]
    row, col = lax.axis_index("row"), lax.axis_index("col")
    zh, x, core = lax.div(row, jnp.int32(X * CORE)), rem(lax.div(row, jnp.int32(CORE)), X), rem(row, CORE)
    way = 2 * core - 1
    turn = rem(zh + dz[0] + dz[1] * way + 2 * ZH - lax.div(col, jnp.int32(2)), ZH)
    low, high = rem(turn, 2), lax.div(turn, jnp.int32(2))
    columns = pl.ds(pl.multiple_of((low * 2 + high) * height, 128), height)
    come = pltpu.make_async_copy(gamma_ref.at[:, columns], old, sems.at[0])
    come.start()
    left, right = [], []
    for array, skip, dx, other_core in places:
        zl, y = rem(core + other_core, CORE), rem(x + dx[0] + dx[1] * way + 2 * X - 2 * high, X)
        left.append(left_ref[y * ZL + rem(zl + lax.div(col, jnp.int32(Y)), ZL)])
        right.append(arrays[array][skip * height : (skip + 1) * height, :])
    commutator = lax.dot_general(
        jnp.concatenate(left, 1),
        jnp.concatenate(right, 1),
        (((1,), (1,)), ((), ())),
        preferred_element_type=jnp.float32,
    )
    come.wait()
    new[...] = (old[...].astype(jnp.float32) + euler_step * commutator).astype(jnp.bfloat16)
    go = pltpu.make_async_copy(new, out_ref.at[:, columns], sems.at[1])
    go.start()
    go.wait()


def block_step(dz, pieces, left, gamma, out):
    arrays = []
    places = []
    for array, skip, dx, core in pieces:
        known = [index for index, had in enumerate(arrays) if had is array]
        if not known:
            known = [len(arrays)]
            arrays.append(array)
        places.append((known[0], skip, dx, core))
    height, count, width = left.shape[1], len(pieces), arrays[0].shape[-1]
    anywhere = pl.BlockSpec(memory_space=pl.ANY)
    operands = [left, *arrays, gamma]
    aliases = {}
    if out is not None:
        aliases = {len(operands): 0}
        operands.append(out)
    return pl.pallas_call(
        functools.partial(block_kernel, dz, places, len(arrays), height),
        in_specs=[
            *[pl.BlockSpec(memory_space=pltpu.VMEM)] * (1 + len(arrays)),
            *[anywhere] * (len(operands) - 1 - len(arrays)),
        ],
        out_specs=anywhere,
        out_shape=jax.ShapeDtypeStruct(gamma.shape, gamma.dtype),
        input_output_aliases=aliases,
        scratch_shapes=[
            pltpu.VMEM((height, height), jnp.bfloat16),
            pltpu.VMEM((height, height), jnp.bfloat16),
            pltpu.SemaphoreType.DMA((2,)),
        ],
        compiler_params=pltpu.CompilerParams(vmem_limit_bytes=20 * 2**20),
        cost_estimate=pl.CostEstimate(
            flops=height * height, bytes_accessed=height * height, transcendentals=0
        ),
        name="block_step",
    )(*operands)


HERE, BACK, AHEAD, ACROSS = (0, 0), (0, 1), (0, -1), (2, 0)


def per_device(eta_ladder, gamma_ladder, occupation, gamma):
    weights = 1.0 - 0.5 * occupation.astype(jnp.float32)
    shard = side_by_side(gamma_ladder, eta_ladder)
    height, width = shard.shape
    other_zl = send(shard, OTHER_ZL)

    p = send(shard, TO_HOME)
    ps = other(p)
    sides = jnp.stack([shard, after(other_zl, ps)])
    alike_y = [[zl * Y + y for y in range(Y)] for zl in range(ZL)]
    gathered = lax.all_gather(sides, "col", axis_index_groups=alike_y).reshape(ZL * Y, height, width)
    xp, xps = send(p, ALONG_X), send(ps, ALONG_X)
    zz = send(jnp.concatenate([p, ps], 0), ALONG_Z)
    fxp = send(xp, ALONG_X)
    zz = after(zz, xps, fxp)
    zs = other(zz)
    z2 = send(zz[:height], ALONG_Z)
    z2s = other(z2)
    xzz, xzs = send(zz, ALONG_X), send(zs, ALONG_X)
    fxzz = send(xzz, ALONG_X)
    xz2, xz2s = send(z2, ALONG_X), send(z2s, ALONG_X)

    left = left_panel_of(after(gathered, z2s), weights)

    def both(arrays, first_core):
        return [
            (array, half, dx, core)
            for array, dx in zip(arrays, (HERE, BACK, AHEAD, ACROSS))
            for half, core in ((0, first_core), (1, 1 - first_core))
        ]

    def alike(mine, swapped, x_mine, x_swapped, their_x, their_x_swapped, fx_mine, their_fx):
        return [
            (mine, 0, HERE, 0),
            (swapped, 0, HERE, 1),
            (x_mine, 0, BACK, 0),
            (x_swapped, 0, BACK, 1),
            (their_x, 0, AHEAD, 1),
            (their_x_swapped, 0, AHEAD, 0),
            (fx_mine, 0, ACROSS, 0),
            (their_fx, 0, ACROSS, 1),
        ]

    out = block_step(HERE, alike(p, ps, xp, xps, other(xp), other(xps), fxp, other(fxp)), left, gamma, None)
    their_fxzz = other(after(fxzz, out))
    out = block_step(BACK, both([zz, xzz, other(xzs), fxzz], 0), left, gamma, out)
    fxz2 = send(after(xz2, out), ALONG_X)
    out = block_step(AHEAD, both([after(zs, xz2s), xzs, other(xzz), their_fxzz], 1), left, gamma, out)
    their_fx = other(after(fxz2, out))
    return block_step(ACROSS, alike(z2, z2s, xz2, xz2s, other(xz2), other(xz2s), fxz2, their_fx), left, gamma, out)


def solution(mesh):
    placed = (P("row", "col"), P("row", "col"), P(), P("row", "col"))
    return jax.shard_map(
        per_device, mesh=mesh, in_specs=placed, out_specs=P("row", "col"), check_vma=False
    )
```

```python
import functools

import jax
import jax.numpy as jnp
from jax import lax
from jax.experimental import pallas as pl
from jax.experimental.pallas import tpu as pltpu
from jax.sharding import PartitionSpec as P

euler_step = 0.5
ZH, X, CORE, ZL, Y = 4, 4, 2, 2, 4
AXES = ("row", "col")


def every_device():
    for zh in range(ZH):
        for x in range(X):
            for core in range(CORE):
                for zl in range(ZL):
                    for y in range(Y):
                        yield zh, x, core, zl, y


def flat(zh, x, core, zl, y):
    return ((((zh % ZH) * X + x % X) * CORE + core % CORE) * ZL + zl % ZL) * Y + y % Y


def home(zh, x, core, zl, y):
    group = zh * 2 + x // 2
    return flat(zh + 2 * core + x % 2, y + 2 * core, zl, group // Y, group % Y)


def pairs(target):
    return [(flat(*d), target(*d)) for d in every_device()]


TO_HOME = pairs(home)
ALONG_Z = pairs(lambda zh, x, core, zl, y: flat(zh + 1 - 2 * core, x, core, zl, y))
ALONG_X = pairs(lambda zh, x, core, zl, y: flat(zh, x + 1 - 2 * core, core, zl, y))
OTHER_ZL = pairs(lambda zh, x, core, zl, y: flat(zh, x, core, zl + 1, y))
OTHER_CORE = pairs(lambda zh, x, core, zl, y: flat(zh, x, core + 1, zl, y))


def send(value, way):
    return lax.ppermute(value, AXES, way)


def other(value):
    return send(value, OTHER_CORE)


def after(value, *earlier):
    return lax.optimization_barrier((value, *earlier))[0]


def weigh(own_ref, other_ref, weights_ref, out_ref):
    half = own_ref.shape[-1] // 2
    k = pl.program_id(0)
    away, y = lax.div(k, jnp.int32(Y)), rem(k, Y)
    side = rem(lax.div(lax.axis_index("col"), jnp.int32(Y)) + away, ZL)
    weights = weights_ref[side * Y + y]

    def put(panel_ref):
        panel = panel_ref[...].astype(jnp.float32)
        out_ref[:, :half] = (panel[:, half:] * weights).astype(jnp.bfloat16)
        out_ref[:, half:] = (panel[:, :half] * weights).astype(jnp.bfloat16)

    pl.when(away == 0)(lambda: put(own_ref))
    pl.when(away == 1)(lambda: put(other_ref))


def left_panel_of(own, others, weights):
    side, height, width = own.shape
    parts = ZL * side
    return pl.pallas_call(
        weigh,
        grid=(parts,),
        in_specs=[
            pl.BlockSpec((None, height, width), lambda k: (jnp.minimum(k, side - 1), 0, 0)),
            pl.BlockSpec((None, height, width), lambda k: (jnp.maximum(k - side, 0), 0, 0)),
            pl.BlockSpec((parts, 1, width // 2), lambda k: (0, 0, 0)),
        ],
        out_specs=pl.BlockSpec((None, height, width), lambda k: (k, 0, 0)),
        out_shape=jax.ShapeDtypeStruct((parts, height, width), jnp.bfloat16),
        compiler_params=pltpu.CompilerParams(vmem_limit_bytes=8 * 2**20),
        cost_estimate=pl.CostEstimate(flops=height, bytes_accessed=height * width, transcendentals=0),
        name="weigh_left",
    )(own, others, weights.reshape(parts, 1, width // 2))


def rem(value, length):
    return lax.rem(value, jnp.int32(length))


def join(left_ref, right_ref, out_ref, sems):
    half = left_ref.shape[-1]
    copies = [
        pltpu.make_async_copy(left_ref, out_ref.at[:, pl.ds(0, half)], sems.at[0]),
        pltpu.make_async_copy(right_ref, out_ref.at[:, pl.ds(half, half)], sems.at[1]),
    ]
    for copy in copies:
        copy.start()
    for copy in copies:
        copy.wait()


def side_by_side(first, second):
    height, width = first.shape
    anywhere = pl.BlockSpec(memory_space=pl.ANY)
    return pl.pallas_call(
        join,
        in_specs=[anywhere, anywhere],
        out_specs=anywhere,
        out_shape=jax.ShapeDtypeStruct((height, 2 * width), first.dtype),
        scratch_shapes=[pltpu.SemaphoreType.DMA((2,))],
        compiler_params=pltpu.CompilerParams(vmem_limit_bytes=4 * 2**20),
        name="join_shard",
    )(first, second)


def block_kernel(dz, places, operands, height, left_ref, *refs):
    arrays, gamma_ref = refs[:operands], refs[operands]
    out_ref, old, new, sems = refs[-4:]
    row, col = lax.axis_index("row"), lax.axis_index("col")
    zh, x, core = lax.div(row, jnp.int32(X * CORE)), rem(lax.div(row, jnp.int32(CORE)), X), rem(row, CORE)
    way = 2 * core - 1
    turn = rem(zh + dz[0] + dz[1] * way + 2 * ZH - lax.div(col, jnp.int32(2)), ZH)
    low, high = rem(turn, 2), lax.div(turn, jnp.int32(2))
    columns = pl.ds(pl.multiple_of((low * 2 + high) * height, 128), height)
    come = pltpu.make_async_copy(gamma_ref.at[:, columns], old, sems.at[0])
    come.start()
    left, right = [], []
    for array, skip, dx, other_core in places:
        zl, y = rem(core + other_core, CORE), rem(x + dx[0] + dx[1] * way + 2 * X - 2 * high, X)
        left.append(left_ref[rem(zl + lax.div(col, jnp.int32(Y)), ZL) * Y + y])
        right.append(arrays[array][skip * height : (skip + 1) * height, :])
    commutator = lax.dot_general(
        jnp.concatenate(left, 1),
        jnp.concatenate(right, 1),
        (((1,), (1,)), ((), ())),
        preferred_element_type=jnp.float32,
    )
    come.wait()
    new[...] = (old[...].astype(jnp.float32) + euler_step * commutator).astype(jnp.bfloat16)
    go = pltpu.make_async_copy(new, out_ref.at[:, columns], sems.at[1])
    go.start()
    go.wait()


def block_step(dz, pieces, left, gamma, out):
    arrays = []
    places = []
    for array, skip, dx, core in pieces:
        known = [index for index, had in enumerate(arrays) if had is array]
        if not known:
            known = [len(arrays)]
            arrays.append(array)
        places.append((known[0], skip, dx, core))
    height, count, width = left.shape[1], len(pieces), arrays[0].shape[-1]
    anywhere = pl.BlockSpec(memory_space=pl.ANY)
    operands = [left, *arrays, gamma]
    aliases = {}
    if out is not None:
        aliases = {len(operands): 0}
        operands.append(out)
    return pl.pallas_call(
        functools.partial(block_kernel, dz, places, len(arrays), height),
        in_specs=[
            *[pl.BlockSpec(memory_space=pltpu.VMEM)] * (1 + len(arrays)),
            *[anywhere] * (len(operands) - 1 - len(arrays)),
        ],
        out_specs=anywhere,
        out_shape=jax.ShapeDtypeStruct(gamma.shape, gamma.dtype),
        input_output_aliases=aliases,
        scratch_shapes=[
            pltpu.VMEM((height, height), jnp.bfloat16),
            pltpu.VMEM((height, height), jnp.bfloat16),
            pltpu.SemaphoreType.DMA((2,)),
        ],
        compiler_params=pltpu.CompilerParams(vmem_limit_bytes=20 * 2**20),
        cost_estimate=pl.CostEstimate(
            flops=height * height, bytes_accessed=height * height, transcendentals=0
        ),
        name="block_step",
    )(*operands)


HERE, BACK, AHEAD, ACROSS = (0, 0), (0, 1), (0, -1), (2, 0)


def per_device(eta_ladder, gamma_ladder, occupation, gamma):
    weights = 1.0 - 0.5 * occupation.astype(jnp.float32)
    shard = side_by_side(gamma_ladder, eta_ladder)
    height = shard.shape[0]
    alike_y = [[zl * Y + y for y in range(Y)] for zl in range(ZL)]
    own = lax.all_gather(shard, "col", axis_index_groups=alike_y)
    other_zl = send(shard, OTHER_ZL)

    p = send(shard, TO_HOME)
    ps = other(p)
    xp, xps = send(p, ALONG_X), send(ps, ALONG_X)
    others = lax.all_gather(after(other_zl, own, xps), "col", axis_index_groups=alike_y)
    zz = send(jnp.concatenate([p, ps], 0), ALONG_Z)
    fxp = send(xp, ALONG_X)
    zz = after(zz, xps, fxp)
    zs = other(zz)
    z2 = send(zz[:height], ALONG_Z)
    xzz, xzs = send(zz, ALONG_X), send(zs, ALONG_X)
    z2 = after(z2, xzz)
    z2s = other(z2)
    fxzz = send(xzz, ALONG_X)
    xz2, xz2s = send(z2, ALONG_X), send(z2s, ALONG_X)

    left = left_panel_of(own, after(others, z2s), weights)

    def both(arrays, first_core):
        return [
            (array, half, dx, core)
            for array, dx in zip(arrays, (HERE, BACK, AHEAD, ACROSS))
            for half, core in ((0, first_core), (1, 1 - first_core))
        ]

    def alike(mine, swapped, x_mine, x_swapped, their_x, their_x_swapped, fx_mine, their_fx):
        return [
            (mine, 0, HERE, 0),
            (swapped, 0, HERE, 1),
            (x_mine, 0, BACK, 0),
            (x_swapped, 0, BACK, 1),
            (their_x, 0, AHEAD, 1),
            (their_x_swapped, 0, AHEAD, 0),
            (fx_mine, 0, ACROSS, 0),
            (their_fx, 0, ACROSS, 1),
        ]

    out = block_step(HERE, alike(p, ps, xp, xps, other(xp), other(xps), fxp, other(fxp)), left, gamma, None)
    their_fxzz = other(after(fxzz, out))
    out = block_step(BACK, both([zz, xzz, other(xzs), fxzz], 0), left, gamma, out)
    fxz2 = send(after(xz2, out), ALONG_X)
    out = block_step(AHEAD, both([after(zs, xz2s), xzs, other(xzz), their_fxzz], 1), left, gamma, out)
    their_fx = other(after(fxz2, out))
    return block_step(ACROSS, alike(z2, z2s, xz2, xz2s, other(xz2), other(xz2s), fxz2, their_fx), left, gamma, out)


def solution(mesh):
    placed = (P("row", "col"), P("row", "col"), P(), P("row", "col"))
    return jax.shard_map(
        per_device, mesh=mesh, in_specs=placed, out_specs=P("row", "col"), check_vma=False
    )
```

```python
import functools

import jax
import jax.numpy as jnp
from jax import lax
from jax.experimental import pallas as pl
from jax.experimental.pallas import tpu as pltpu
from jax.sharding import PartitionSpec as P

euler_step = 0.5
ZH, X, CORE, ZL, Y = 4, 4, 2, 2, 4
AXES = ("row", "col")


def every_device():
    for zh in range(ZH):
        for x in range(X):
            for core in range(CORE):
                for zl in range(ZL):
                    for y in range(Y):
                        yield zh, x, core, zl, y


def flat(zh, x, core, zl, y):
    return ((((zh % ZH) * X + x % X) * CORE + core % CORE) * ZL + zl % ZL) * Y + y % Y


def home(zh, x, core, zl, y):
    group = zh * 2 + x // 2
    return flat(zh + 2 * core + x % 2, y + 2 * core, zl, group // Y, group % Y)


def pairs(target):
    return [(flat(*d), target(*d)) for d in every_device()]


TO_HOME = pairs(home)
ALONG_Z = pairs(lambda zh, x, core, zl, y: flat(zh + 1 - 2 * core, x, core, zl, y))
ALONG_X = pairs(lambda zh, x, core, zl, y: flat(zh, x + 1 - 2 * core, core, zl, y))
OTHER_ZL = pairs(lambda zh, x, core, zl, y: flat(zh, x, core, zl + 1, y))
OTHER_CORE = pairs(lambda zh, x, core, zl, y: flat(zh, x, core + 1, zl, y))


def send(value, way):
    return lax.ppermute(value, AXES, way)


def other(value):
    return send(value, OTHER_CORE)


def after(value, *earlier):
    return lax.optimization_barrier((value, *earlier))[0]


def weigh(own_ref, other_ref, weights_ref, out_ref):
    half = own_ref.shape[-1] // 2
    k = pl.program_id(0)
    away, y = lax.div(k, jnp.int32(Y)), rem(k, Y)
    side = rem(lax.div(lax.axis_index("col"), jnp.int32(Y)) + away, ZL)
    weights = weights_ref[side * Y + y]

    def put(panel_ref):
        panel = panel_ref[...].astype(jnp.float32)
        out_ref[:, :half] = (panel[:, half:] * weights).astype(jnp.bfloat16)
        out_ref[:, half:] = (panel[:, :half] * weights).astype(jnp.bfloat16)

    pl.when(away == 0)(lambda: put(own_ref))
    pl.when(away == 1)(lambda: put(other_ref))


def left_panel_of(own, others, weights):
    side, height, width = own.shape
    parts = ZL * side
    return pl.pallas_call(
        weigh,
        grid=(parts,),
        in_specs=[
            pl.BlockSpec((None, height, width), lambda k: (jnp.minimum(k, side - 1), 0, 0)),
            pl.BlockSpec((None, height, width), lambda k: (jnp.maximum(k - side, 0), 0, 0)),
            pl.BlockSpec((parts, 1, width // 2), lambda k: (0, 0, 0)),
        ],
        out_specs=pl.BlockSpec((None, height, width), lambda k: (k, 0, 0)),
        out_shape=jax.ShapeDtypeStruct((parts, height, width), jnp.bfloat16),
        compiler_params=pltpu.CompilerParams(vmem_limit_bytes=8 * 2**20),
        cost_estimate=pl.CostEstimate(flops=height, bytes_accessed=height * width, transcendentals=0),
        name="weigh_left",
    )(own, others, weights.reshape(parts, 1, width // 2))


def rem(value, length):
    return lax.rem(value, jnp.int32(length))


def join(left_ref, right_ref, out_ref, sems):
    half = left_ref.shape[-1]
    copies = [
        pltpu.make_async_copy(left_ref, out_ref.at[:, pl.ds(0, half)], sems.at[0]),
        pltpu.make_async_copy(right_ref, out_ref.at[:, pl.ds(half, half)], sems.at[1]),
    ]
    for copy in copies:
        copy.start()
    for copy in copies:
        copy.wait()


def side_by_side(first, second):
    height, width = first.shape
    anywhere = pl.BlockSpec(memory_space=pl.ANY)
    return pl.pallas_call(
        join,
        in_specs=[anywhere, anywhere],
        out_specs=anywhere,
        out_shape=jax.ShapeDtypeStruct((height, 2 * width), first.dtype),
        scratch_shapes=[pltpu.SemaphoreType.DMA((2,))],
        compiler_params=pltpu.CompilerParams(vmem_limit_bytes=4 * 2**20),
        name="join_shard",
    )(first, second)


def block_kernel(blocks, operands, height, left_ref, *refs):
    arrays, gamma_ref = refs[:operands], refs[operands]
    out_ref, old, new, sems = refs[-4:]
    row, col = lax.axis_index("row"), lax.axis_index("col")
    zh, x, core = lax.div(row, jnp.int32(X * CORE)), rem(lax.div(row, jnp.int32(CORE)), X), rem(row, CORE)
    way = 2 * core - 1

    def turn_of(dz):
        turn = rem(zh + dz[0] + dz[1] * way + 2 * ZH - lax.div(col, jnp.int32(2)), ZH)
        return rem(turn, 2), lax.div(turn, jnp.int32(2))

    columns, coming = [], []
    for index, (dz, _) in enumerate(blocks):
        low, high = turn_of(dz)
        columns.append(pl.ds(pl.multiple_of((low * 2 + high) * height, 128), height))
        here = old.at[:, pl.ds(index * height, height)]
        coming.append(pltpu.make_async_copy(gamma_ref.at[:, columns[index]], here, sems.at[index]))
        coming[index].start()
    high = turn_of(blocks[0][0])[1]
    left, right = [], []
    for place in range(len(blocks[0][1])):
        _, _, dx, other_core = blocks[0][1][place]
        zl, y = rem(core + other_core, CORE), rem(x + dx[0] + dx[1] * way + 2 * X - 2 * high, X)
        left.append(left_ref[rem(zl + lax.div(col, jnp.int32(Y)), ZL) * Y + y])
        halves = [(arrays[pieces[place][0]], pieces[place][1]) for _, pieces in blocks]
        right.append(jnp.concatenate([array[skip * height : (skip + 1) * height, :] for array, skip in halves], 0))
    left, right = jnp.concatenate(left, 1), jnp.concatenate(right, 1)
    total = len(blocks) * height
    going = []
    for first in range(0, total, 512):
        last = min(first + 512, total)
        commutator = lax.dot_general(
            left, right[first:last], (((1,), (1,)), ((), ())), preferred_element_type=jnp.float32
        )
        if first == 0:
            for copy in coming:
                copy.wait()
        new[:, first:last] = (old[:, first:last].astype(jnp.float32) + euler_step * commutator).astype(jnp.bfloat16)
        while (len(going) + 1) * height <= last:
            index = len(going)
            there = out_ref.at[:, columns[index]]
            going.append(pltpu.make_async_copy(new.at[:, pl.ds(index * height, height)], there, sems.at[len(blocks) + index]))
            going[index].start()
    for copy in going:
        copy.wait()


def block_step(blocks, left, gamma, out):
    arrays = []
    placed = []
    for dz, pieces in blocks:
        places = []
        for array, skip, dx, core in pieces:
            known = [index for index, had in enumerate(arrays) if had is array]
            if not known:
                known = [len(arrays)]
                arrays.append(array)
            places.append((known[0], skip, dx, core))
        placed.append((dz, places))
    height, width = left.shape[1], left.shape[0] * left.shape[2]
    anywhere = pl.BlockSpec(memory_space=pl.ANY)
    operands = [left, *arrays, gamma]
    aliases = {}
    if out is not None:
        aliases = {len(operands): 0}
        operands.append(out)
    return pl.pallas_call(
        functools.partial(block_kernel, placed, len(arrays), height),
        in_specs=[
            *[pl.BlockSpec(memory_space=pltpu.VMEM)] * (1 + len(arrays)),
            *[anywhere] * (len(operands) - 1 - len(arrays)),
        ],
        out_specs=anywhere,
        out_shape=jax.ShapeDtypeStruct(gamma.shape, gamma.dtype),
        input_output_aliases=aliases,
        scratch_shapes=[
            pltpu.VMEM((height, len(blocks) * height), jnp.bfloat16),
            pltpu.VMEM((height, len(blocks) * height), jnp.bfloat16),
            pltpu.SemaphoreType.DMA((2 * len(blocks),)),
        ],
        compiler_params=pltpu.CompilerParams(vmem_limit_bytes=28 * 2**20),
        cost_estimate=pl.CostEstimate(flops=height * height, bytes_accessed=height * height, transcendentals=0),
        name="block_step",
    )(*operands)


HERE, BACK, AHEAD, ACROSS = (0, 0), (0, 1), (0, -1), (2, 0)


def per_device(eta_ladder, gamma_ladder, occupation, gamma):
    weights = 1.0 - 0.5 * occupation.astype(jnp.float32)
    shard = side_by_side(gamma_ladder, eta_ladder)
    height = shard.shape[0]
    alike_y = [[zl * Y + y for y in range(Y)] for zl in range(ZL)]
    own = lax.all_gather(shard, "col", axis_index_groups=alike_y)

    p = send(shard, TO_HOME)
    other_zl = send(shard, OTHER_ZL)
    p = after(p, other_zl)
    p = jnp.concatenate([p, other(p)], 0)
    xp = send(p, ALONG_X)
    others = lax.all_gather(after(other_zl, own, xp), "col", axis_index_groups=alike_y)
    fxp = send(xp[:height], ALONG_X)
    zz = after(send(p, ALONG_Z), fxp)
    zs = other(zz)
    z2 = send(zz[:height], ALONG_Z)
    xzz, xzs = send(zz, ALONG_X), send(zs, ALONG_X)
    fxzz = send(xzz, ALONG_X)
    z2 = jnp.concatenate([z2, other(z2)], 0)
    xz2 = send(z2, ALONG_X)

    left = left_panel_of(own, after(others, z2), weights)

    def pieces(here, back, ahead, across, first_cores):
        parts = [(here, HERE), (back, BACK), (ahead, AHEAD), (across, ACROSS)]
        out = []
        for (arrays, dx), first_core in zip(parts, first_cores):
            arrays = arrays if isinstance(arrays, tuple) else (arrays, arrays)
            halves = [0, 0] if arrays[0] is not arrays[1] else [0, 1]
            order = [0, 1] if first_core == 0 else [1, 0]
            out.append([(arrays[i], halves[i], dx, core) for core, i in enumerate(order)])
        return out

    def flat_list(groups, turned):
        order = [3, 2, 1, 0] if turned else [0, 1, 2, 3]
        return [piece for index in order for piece in groups[index]]

    near = flat_list(pieces(zz, xzz, other(xzs), fxzz, (0, 0, 0, 0)), False)
    far = flat_list(pieces(zs, xzs, other(xzz), other(fxzz), (1, 1, 1, 1)), True)
    out = block_step([(BACK, near), (AHEAD, far)], left, gamma, None)
    fxz2 = send(xz2[:height], ALONG_X)
    same = flat_list(pieces(p, xp, other(xp), (fxp, other(fxp)), (0, 0, 1, 0)), False)
    last = flat_list(pieces(z2, xz2, other(xz2), (fxz2, other(after(fxz2, out))), (0, 0, 1, 0)), True)
    return block_step([(HERE, same), (ACROSS, last)], left, gamma, out)


def solution(mesh):
    placed = (P("row", "col"), P("row", "col"), P(), P("row", "col"))
    return jax.shard_map(
        per_device, mesh=mesh, in_specs=placed, out_specs=P("row", "col"), check_vma=False
    )
```

```python
import functools

import jax
import jax.numpy as jnp
from jax import lax
from jax.experimental import pallas as pl
from jax.experimental.pallas import tpu as pltpu
from jax.sharding import PartitionSpec as P

euler_step = 0.5
ZH, X, CORE, ZL, Y = 4, 4, 2, 2, 4
AXES = ("row", "col")


def every_device():
    for zh in range(ZH):
        for x in range(X):
            for core in range(CORE):
                for zl in range(ZL):
                    for y in range(Y):
                        yield zh, x, core, zl, y


def flat(zh, x, core, zl, y):
    return ((((zh % ZH) * X + x % X) * CORE + core % CORE) * ZL + zl % ZL) * Y + y % Y


def home(zh, x, core, zl, y):
    group = zh * 2 + x // 2
    return flat(zh + 2 * core + x % 2, y + 2 * core, zl, group // Y, group % Y)


def pairs(target):
    return [(flat(*d), target(*d)) for d in every_device()]


TO_HOME = pairs(home)
ALONG_Z = pairs(lambda zh, x, core, zl, y: flat(zh + 1 - 2 * core, x, core, zl, y))
ALONG_X = pairs(lambda zh, x, core, zl, y: flat(zh, x + 1 - 2 * core, core, zl, y))
OTHER_ZL = pairs(lambda zh, x, core, zl, y: flat(zh, x, core, zl + 1, y))
OTHER_CORE = pairs(lambda zh, x, core, zl, y: flat(zh, x, core + 1, zl, y))


def send(value, way):
    return lax.ppermute(value, AXES, way)


def other(value):
    return send(value, OTHER_CORE)


def after(value, *earlier):
    return lax.optimization_barrier((value, *earlier))[0]


def weigh(own_ref, other_ref, weights_ref, out_ref):
    half = own_ref.shape[-1] // 2
    k = pl.program_id(0)
    away, y = lax.div(k, jnp.int32(Y)), rem(k, Y)
    side = rem(lax.div(lax.axis_index("col"), jnp.int32(Y)) + away, ZL)
    weights = weights_ref[side * Y + y]

    def put(panel_ref):
        panel = panel_ref[...].astype(jnp.float32)
        out_ref[:, :half] = (panel[:, half:] * weights).astype(jnp.bfloat16)
        out_ref[:, half:] = (panel[:, :half] * weights).astype(jnp.bfloat16)

    pl.when(away == 0)(lambda: put(own_ref))
    pl.when(away == 1)(lambda: put(other_ref))


def left_panel_of(own, others, weights):
    side, height, width = own.shape
    parts = ZL * side
    return pl.pallas_call(
        weigh,
        grid=(parts,),
        in_specs=[
            pl.BlockSpec((None, height, width), lambda k: (jnp.minimum(k, side - 1), 0, 0)),
            pl.BlockSpec((None, height, width), lambda k: (jnp.maximum(k - side, 0), 0, 0)),
            pl.BlockSpec((parts, 1, width // 2), lambda k: (0, 0, 0)),
        ],
        out_specs=pl.BlockSpec((None, height, width), lambda k: (k, 0, 0)),
        out_shape=jax.ShapeDtypeStruct((parts, height, width), jnp.bfloat16),
        compiler_params=pltpu.CompilerParams(vmem_limit_bytes=8 * 2**20),
        cost_estimate=pl.CostEstimate(flops=height, bytes_accessed=height * width, transcendentals=0),
        name="weigh_left",
    )(own, others, weights.reshape(parts, 1, width // 2))


def rem(value, length):
    return lax.rem(value, jnp.int32(length))


def join(left_ref, right_ref, out_ref, sems):
    half = left_ref.shape[-1]
    copies = [
        pltpu.make_async_copy(left_ref, out_ref.at[:, pl.ds(0, half)], sems.at[0]),
        pltpu.make_async_copy(right_ref, out_ref.at[:, pl.ds(half, half)], sems.at[1]),
    ]
    for copy in copies:
        copy.start()
    for copy in copies:
        copy.wait()


def side_by_side(first, second):
    height, width = first.shape
    anywhere = pl.BlockSpec(memory_space=pl.ANY)
    return pl.pallas_call(
        join,
        in_specs=[anywhere, anywhere],
        out_specs=anywhere,
        out_shape=jax.ShapeDtypeStruct((height, 2 * width), first.dtype),
        scratch_shapes=[pltpu.SemaphoreType.DMA((2,))],
        compiler_params=pltpu.CompilerParams(vmem_limit_bytes=4 * 2**20),
        name="join_shard",
    )(first, second)


def block_kernel(blocks, operands, height, left_ref, *refs):
    arrays, gamma_ref = refs[:operands], refs[operands]
    out_ref, right, total, old, new, sems = refs[-6:]
    row, col = lax.axis_index("row"), lax.axis_index("col")
    zh, x, core = lax.div(row, jnp.int32(X * CORE)), rem(lax.div(row, jnp.int32(CORE)), X), rem(row, CORE)
    way = 2 * core - 1

    def turn_of(dz):
        turn = rem(zh + dz[0] + dz[1] * way + 2 * ZH - lax.div(col, jnp.int32(2)), ZH)
        return rem(turn, 2), lax.div(turn, jnp.int32(2))

    count, width = len(blocks[0][1]), arrays[0].shape[-1]
    phases = 2
    arriving = [[] for _ in range(phases)]
    for place in range(count):
        for index, (_, pieces) in enumerate(blocks):
            array, skip = pieces[place][:2]
            arriving[place * phases // count].append(
                pltpu.make_async_copy(
                    arrays[array].at[pl.ds(skip * height, height), :],
                    right.at[pl.ds(index * height, height), pl.ds(place * width, width)],
                    sems.at[place * len(blocks) + index],
                )
            )
    columns = []
    for index, (dz, _) in enumerate(blocks):
        low, high = turn_of(dz)
        columns.append(pl.ds(pl.multiple_of((low * 2 + high) * height, 128), height))
        here = old.at[:, pl.ds(index * height, height)]
        copy = pltpu.make_async_copy(gamma_ref.at[:, columns[index]], here, sems.at[count * len(blocks) + index])
        arriving[-1].append(copy)
    for copies in arriving:
        for copy in copies:
            copy.start()
    high = turn_of(blocks[0][0])[1]
    left = []
    for place in range(count):
        _, _, dx, other_core = blocks[0][1][place]
        zl, y = rem(core + other_core, CORE), rem(x + dx[0] + dx[1] * way + 2 * X - 2 * high, X)
        left.append(left_ref[rem(zl + lax.div(col, jnp.int32(Y)), ZL) * Y + y])
    all_columns = len(blocks) * height
    going = []
    for phase, copies in enumerate(arriving):
        for copy in copies:
            copy.wait()
        depth = count // phases
        mine = jnp.concatenate(left[phase * depth : (phase + 1) * depth], 1)
        for first in range(0, all_columns, 512):
            last = min(first + 512, all_columns)
            commutator = lax.dot_general(
                mine,
                right[first:last, phase * depth * width : (phase + 1) * depth * width],
                (((1,), (1,)), ((), ())),
                preferred_element_type=jnp.float32,
            )
            if phase > 0:
                commutator = total[:, first:last] + commutator
            if phase < phases - 1:
                total[:, first:last] = commutator
                continue
            new[:, first:last] = (old[:, first:last].astype(jnp.float32) + euler_step * commutator).astype(jnp.bfloat16)
            while (len(going) + 1) * height <= last:
                index = len(going)
                there, sem = out_ref.at[:, columns[index]], sems.at[(count + 1) * len(blocks) + index]
                going.append(pltpu.make_async_copy(new.at[:, pl.ds(index * height, height)], there, sem))
                going[index].start()
    for copy in going:
        copy.wait()


def block_step(blocks, left, gamma, out):
    arrays = []
    placed = []
    for dz, pieces in blocks:
        places = []
        for array, skip, dx, core in pieces:
            known = [index for index, had in enumerate(arrays) if had is array]
            if not known:
                known = [len(arrays)]
                arrays.append(array)
            places.append((known[0], skip, dx, core))
        placed.append((dz, places))
    height, width = left.shape[1], left.shape[0] * left.shape[2]
    anywhere = pl.BlockSpec(memory_space=pl.ANY)
    operands = [left, *arrays, gamma]
    aliases = {}
    if out is not None:
        aliases = {len(operands): 0}
        operands.append(out)
    return pl.pallas_call(
        functools.partial(block_kernel, placed, len(arrays), height),
        in_specs=[
            pl.BlockSpec(memory_space=pltpu.VMEM),
            *[anywhere] * (len(operands) - 1),
        ],
        out_specs=anywhere,
        out_shape=jax.ShapeDtypeStruct(gamma.shape, gamma.dtype),
        input_output_aliases=aliases,
        scratch_shapes=[
            pltpu.VMEM((len(blocks) * height, width), jnp.bfloat16),
            pltpu.VMEM((height, len(blocks) * height), jnp.float32),
            pltpu.VMEM((height, len(blocks) * height), jnp.bfloat16),
            pltpu.VMEM((height, len(blocks) * height), jnp.bfloat16),
            pltpu.SemaphoreType.DMA(((len(blocks[0][1]) + 2) * len(blocks),)),
        ],
        compiler_params=pltpu.CompilerParams(vmem_limit_bytes=28 * 2**20),
        cost_estimate=pl.CostEstimate(flops=height * height, bytes_accessed=height * height, transcendentals=0),
        name="block_step",
    )(*operands)


HERE, BACK, AHEAD, ACROSS = (0, 0), (0, 1), (0, -1), (2, 0)


def per_device(eta_ladder, gamma_ladder, occupation, gamma):
    weights = 1.0 - 0.5 * occupation.astype(jnp.float32)
    shard = side_by_side(gamma_ladder, eta_ladder)
    height = shard.shape[0]
    alike_y = [[zl * Y + y for y in range(Y)] for zl in range(ZL)]
    own = lax.all_gather(shard, "col", axis_index_groups=alike_y)

    p = send(shard, TO_HOME)
    other_zl = send(shard, OTHER_ZL)
    p = after(p, other_zl)
    ps = other(p)
    za, zb = send(p, ALONG_Z), send(ps, ALONG_Z)
    xp, xps = send(p, ALONG_X), send(ps, ALONG_X)
    others = lax.all_gather(after(other_zl, own, xp), "col", axis_index_groups=alike_y)
    fxp = send(after(xp, xps), ALONG_X)
    z2 = send(za, ALONG_Z)
    zz = jnp.concatenate([za, after(zb, xps, fxp)], 0)
    zs = other(zz)
    xzz, xzs = send(zz, ALONG_X), send(zs, ALONG_X)
    fxzz = send(after(xzz, z2), ALONG_X)
    z2s = other(z2)
    xz2, xz2s = send(z2, ALONG_X), send(z2s, ALONG_X)

    left = left_panel_of(own, after(others, z2s), weights)

    def singles(here, back, ahead, across):
        return list(zip((*here, *back, *ahead, *across), [0] * 8, [HERE] * 2 + [BACK] * 2 + [AHEAD] * 2 + [ACROSS] * 2, [0, 1] * 4))

    def pairs_of(arrays, first_core):
        return [
            (array, core ^ first_core, dx, core)
            for array, dx in zip(arrays, (HERE, BACK, AHEAD, ACROSS))
            for core in (0, 1)
        ]

    def turned(pieces):
        return [piece for index in (3, 2, 1, 0) for piece in pieces[2 * index : 2 * index + 2]]

    fxz2 = send(xz2, ALONG_X)
    near = pairs_of([zz, xzz, other(xzs), fxzz], 0)
    far = pairs_of([zs, xzs, other(xzz), other(after(fxzz, xz2, xz2s))], 1)
    out = block_step([(BACK, near), (AHEAD, turned(far))], left, gamma, None)
    their_fxz2 = other(after(fxz2, out))
    same = singles((p, ps), (xp, xps), (other(xps), other(xp)), (fxp, other(fxp)))
    last = singles((z2, z2s), (xz2, xz2s), (other(xz2s), other(xz2)), (fxz2, their_fxz2))
    return block_step([(HERE, same), (ACROSS, turned(last))], left, gamma, out)


def solution(mesh):
    placed = (P("row", "col"), P("row", "col"), P(), P("row", "col"))
    return jax.shard_map(
        per_device, mesh=mesh, in_specs=placed, out_specs=P("row", "col"), check_vma=False
    )
```

```python
import functools

import jax
import jax.numpy as jnp
from jax import lax
from jax.experimental import pallas as pl
from jax.experimental.pallas import tpu as pltpu
from jax.sharding import PartitionSpec as P

euler_step = 0.5
ZH, X, CORE, ZL, Y = 4, 4, 2, 2, 4
AXES = ("row", "col")


def every_device():
    for zh in range(ZH):
        for x in range(X):
            for core in range(CORE):
                for zl in range(ZL):
                    for y in range(Y):
                        yield zh, x, core, zl, y


def flat(zh, x, core, zl, y):
    return ((((zh % ZH) * X + x % X) * CORE + core % CORE) * ZL + zl % ZL) * Y + y % Y


def home(zh, x, core, zl, y, step=0):
    group = zh * 2 + x // 2
    return flat(zh + 2 * core + x % 2 + step, y + 2 * core + step, zl, group // Y, group % Y)


def pairs(target):
    return [(flat(*d), target(*d)) for d in every_device()]


TO_HOME = pairs(home)
TO_SECOND = pairs(lambda *device: home(*device, step=2))
ALONG_Z = pairs(lambda zh, x, core, zl, y: flat(zh + 1 - 2 * core, x, core, zl, y))
ALONG_X = pairs(lambda zh, x, core, zl, y: flat(zh, x + 1 - 2 * core, core, zl, y))
OTHER_ZL = pairs(lambda zh, x, core, zl, y: flat(zh, x, core, zl + 1, y))
OTHER_CORE = pairs(lambda zh, x, core, zl, y: flat(zh, x, core + 1, zl, y))


def send(value, way):
    return lax.ppermute(value, AXES, way)


def other(value):
    return send(value, OTHER_CORE)


def after(value, *earlier):
    return lax.optimization_barrier((value, *earlier))[0]


def weigh(own_ref, other_ref, weights_ref, out_ref):
    half = own_ref.shape[-1] // 2
    k = pl.program_id(0)
    away, y = lax.div(k, jnp.int32(Y)), rem(k, Y)
    side = rem(lax.div(lax.axis_index("col"), jnp.int32(Y)) + away, ZL)
    weights = weights_ref[side * Y + y]

    def put(panel_ref):
        panel = panel_ref[...].astype(jnp.float32)
        out_ref[:, :half] = (panel[:, half:] * weights).astype(jnp.bfloat16)
        out_ref[:, half:] = (panel[:, :half] * weights).astype(jnp.bfloat16)

    pl.when(away == 0)(lambda: put(own_ref))
    pl.when(away == 1)(lambda: put(other_ref))


def left_panel_of(own, others, weights):
    side, height, width = own.shape
    parts = ZL * side
    return pl.pallas_call(
        weigh,
        grid=(parts,),
        in_specs=[
            pl.BlockSpec((None, height, width), lambda k: (jnp.minimum(k, side - 1), 0, 0)),
            pl.BlockSpec((None, height, width), lambda k: (jnp.maximum(k - side, 0), 0, 0)),
            pl.BlockSpec((parts, 1, width // 2), lambda k: (0, 0, 0)),
        ],
        out_specs=pl.BlockSpec((None, height, width), lambda k: (k, 0, 0)),
        out_shape=jax.ShapeDtypeStruct((parts, height, width), jnp.bfloat16),
        compiler_params=pltpu.CompilerParams(vmem_limit_bytes=8 * 2**20),
        cost_estimate=pl.CostEstimate(flops=height, bytes_accessed=height * width, transcendentals=0),
        name="weigh_left",
    )(own, others, weights.reshape(parts, 1, width // 2))


def rem(value, length):
    return lax.rem(value, jnp.int32(length))


def join(left_ref, right_ref, out_ref, sems):
    half = left_ref.shape[-1]
    copies = [
        pltpu.make_async_copy(left_ref, out_ref.at[:, pl.ds(0, half)], sems.at[0]),
        pltpu.make_async_copy(right_ref, out_ref.at[:, pl.ds(half, half)], sems.at[1]),
    ]
    for copy in copies:
        copy.start()
    for copy in copies:
        copy.wait()


def side_by_side(first, second):
    height, width = first.shape
    anywhere = pl.BlockSpec(memory_space=pl.ANY)
    return pl.pallas_call(
        join,
        in_specs=[anywhere, anywhere],
        out_specs=anywhere,
        out_shape=jax.ShapeDtypeStruct((height, 2 * width), first.dtype),
        scratch_shapes=[pltpu.SemaphoreType.DMA((2,))],
        compiler_params=pltpu.CompilerParams(vmem_limit_bytes=4 * 2**20),
        name="join_shard",
    )(first, second)


def block_kernel(blocks, operands, height, left_ref, *refs):
    arrays, gamma_ref = refs[:operands], refs[operands]
    out_ref, right, total, old, new, sems = refs[-6:]
    row, col = lax.axis_index("row"), lax.axis_index("col")
    zh, x, core = lax.div(row, jnp.int32(X * CORE)), rem(lax.div(row, jnp.int32(CORE)), X), rem(row, CORE)
    way = 2 * core - 1

    def turn_of(dz):
        turn = rem(zh + dz[0] + dz[1] * way + 2 * ZH - lax.div(col, jnp.int32(2)), ZH)
        return rem(turn, 2), lax.div(turn, jnp.int32(2))

    count, width = len(blocks[0][1]), arrays[0].shape[-1]
    phases = 2
    arriving = [[] for _ in range(phases)]
    for place in range(count):
        for index, (_, pieces) in enumerate(blocks):
            array, skip = pieces[place][:2]
            arriving[place * phases // count].append(
                pltpu.make_async_copy(
                    arrays[array].at[pl.ds(skip * height, height), :],
                    right.at[pl.ds(index * height, height), pl.ds(place * width, width)],
                    sems.at[place * len(blocks) + index],
                )
            )
    columns = []
    for index, (dz, _) in enumerate(blocks):
        low, high = turn_of(dz)
        columns.append(pl.ds(pl.multiple_of((low * 2 + high) * height, 128), height))
        here = old.at[:, pl.ds(index * height, height)]
        copy = pltpu.make_async_copy(gamma_ref.at[:, columns[index]], here, sems.at[count * len(blocks) + index])
        arriving[-1].append(copy)
    for copies in arriving:
        for copy in copies:
            copy.start()
    high = turn_of(blocks[0][0])[1]
    left = []
    for place in range(count):
        _, _, dx, other_core = blocks[0][1][place]
        zl, y = rem(core + other_core, CORE), rem(x + dx[0] + dx[1] * way + 2 * X - 2 * high, X)
        left.append(left_ref[rem(zl + lax.div(col, jnp.int32(Y)), ZL) * Y + y])
    all_columns = len(blocks) * height
    going = []
    for phase, copies in enumerate(arriving):
        for copy in copies:
            copy.wait()
        depth = count // phases
        mine = jnp.concatenate(left[phase * depth : (phase + 1) * depth], 1)
        for first in range(0, all_columns, 512):
            last = min(first + 512, all_columns)
            commutator = lax.dot_general(
                mine,
                right[first:last, phase * depth * width : (phase + 1) * depth * width],
                (((1,), (1,)), ((), ())),
                preferred_element_type=jnp.float32,
            )
            if phase > 0:
                commutator = total[:, first:last] + commutator
            if phase < phases - 1:
                total[:, first:last] = commutator
                continue
            new[:, first:last] = (old[:, first:last].astype(jnp.float32) + euler_step * commutator).astype(jnp.bfloat16)
            while (len(going) + 1) * height <= last:
                index = len(going)
                there, sem = out_ref.at[:, columns[index]], sems.at[(count + 1) * len(blocks) + index]
                going.append(pltpu.make_async_copy(new.at[:, pl.ds(index * height, height)], there, sem))
                going[index].start()
    for copy in going:
        copy.wait()


def block_step(blocks, left, gamma, out):
    arrays = []
    placed = []
    for dz, pieces in blocks:
        places = []
        for array, skip, dx, core in pieces:
            known = [index for index, had in enumerate(arrays) if had is array]
            if not known:
                known = [len(arrays)]
                arrays.append(array)
            places.append((known[0], skip, dx, core))
        placed.append((dz, places))
    height, width = left.shape[1], left.shape[0] * left.shape[2]
    anywhere = pl.BlockSpec(memory_space=pl.ANY)
    operands = [left, *arrays, gamma]
    aliases = {}
    if out is not None:
        aliases = {len(operands): 0}
        operands.append(out)
    return pl.pallas_call(
        functools.partial(block_kernel, placed, len(arrays), height),
        in_specs=[
            pl.BlockSpec(memory_space=pltpu.VMEM),
            *[anywhere] * (len(operands) - 1),
        ],
        out_specs=anywhere,
        out_shape=jax.ShapeDtypeStruct(gamma.shape, gamma.dtype),
        input_output_aliases=aliases,
        scratch_shapes=[
            pltpu.VMEM((len(blocks) * height, width), jnp.bfloat16),
            pltpu.VMEM((height, len(blocks) * height), jnp.float32),
            pltpu.VMEM((height, len(blocks) * height), jnp.bfloat16),
            pltpu.VMEM((height, len(blocks) * height), jnp.bfloat16),
            pltpu.SemaphoreType.DMA(((len(blocks[0][1]) + 2) * len(blocks),)),
        ],
        compiler_params=pltpu.CompilerParams(vmem_limit_bytes=28 * 2**20),
        cost_estimate=pl.CostEstimate(flops=height * height, bytes_accessed=height * height, transcendentals=0),
        name="block_step",
    )(*operands)


HERE, BACK, AHEAD, ACROSS = (0, 0), (0, 1), (0, -1), (2, 0)


def per_device(eta_ladder, gamma_ladder, occupation, gamma):
    weights = 1.0 - 0.5 * occupation.astype(jnp.float32)
    shard = side_by_side(gamma_ladder, eta_ladder)
    height = shard.shape[0]
    alike_y = [[zl * Y + y for y in range(Y)] for zl in range(ZL)]
    own = lax.all_gather(shard, "col", axis_index_groups=alike_y)

    p, p2 = send(shard, TO_HOME), send(shard, TO_SECOND)
    other_zl = send(shard, OTHER_ZL)
    p = jnp.concatenate([p, after(p2, other_zl)], 0)
    ps = other(p)
    xp, xps = send(p, ALONG_X), send(ps, ALONG_X)
    fxp = send(xp, ALONG_X)
    zz = after(send(p, ALONG_Z), xps)
    others = lax.all_gather(after(other_zl, own, ps), "col", axis_index_groups=alike_y)
    zs = other(zz)
    xzz, xzs = send(zz, ALONG_X), send(zs, ALONG_X)
    fxzz = send(xzz, ALONG_X)
    left = left_panel_of(own, others, weights)

    def places(entries, half):
        return [(array, half ^ turn, (dx[0] + 2 * (half ^ turn), dx[1]), core) for array, turn, dx, core in entries]

    alike = [
        (p, 0, HERE, 0),
        (ps, 0, HERE, 1),
        (xp, 0, BACK, 0),
        (xps, 0, BACK, 1),
        (other(xp), 0, AHEAD, 1),
        (other(xps), 0, AHEAD, 0),
        (fxp, 0, ACROSS, 0),
        (other(fxp), 0, ACROSS, 1),
    ]
    out = block_step([(HERE, places(alike, 0)), (ACROSS, places(alike, 1))], left, gamma, None)
    between = [
        (zz, 0, HERE, 0),
        (zs, 1, HERE, 1),
        (xzz, 0, BACK, 0),
        (xzs, 1, BACK, 1),
        (other(xzz), 1, AHEAD, 1),
        (other(xzs), 0, AHEAD, 0),
        (fxzz, 0, ACROSS, 0),
        (other(after(fxzz, out)), 1, ACROSS, 1),
    ]
    return block_step([(BACK, places(between, 0)), (AHEAD, places(between, 1))], left, gamma, out)


def solution(mesh):
    placed = (P("row", "col"), P("row", "col"), P(), P("row", "col"))
    return jax.shard_map(
        per_device, mesh=mesh, in_specs=placed, out_specs=P("row", "col"), check_vma=False
    )
```

```python
import functools

import jax
import jax.numpy as jnp
from jax import lax
from jax.experimental import pallas as pl
from jax.experimental.pallas import tpu as pltpu
from jax.sharding import PartitionSpec as P

euler_step = 0.5
ZH, X, CORE, ZL, Y = 4, 4, 2, 2, 4
AXES = ("row", "col")


def every_device():
    for zh in range(ZH):
        for x in range(X):
            for core in range(CORE):
                for zl in range(ZL):
                    for y in range(Y):
                        yield zh, x, core, zl, y


def flat(zh, x, core, zl, y):
    return ((((zh % ZH) * X + x % X) * CORE + core % CORE) * ZL + zl % ZL) * Y + y % Y


def home(zh, x, core, zl, y):
    group = zh * 2 + x // 2
    return flat(zh + 2 * core + x % 2, y + 2 * core, zl, group // Y, group % Y)


def pairs(target):
    return [(flat(*d), target(*d)) for d in every_device()]


TO_HOME = pairs(home)
ALONG_Z = pairs(lambda zh, x, core, zl, y: flat(zh + 1 - 2 * core, x, core, zl, y))
ALONG_X = pairs(lambda zh, x, core, zl, y: flat(zh, x + 1 - 2 * core, core, zl, y))
OTHER_ZL = pairs(lambda zh, x, core, zl, y: flat(zh, x, core, zl + 1, y))
OTHER_CORE = pairs(lambda zh, x, core, zl, y: flat(zh, x, core + 1, zl, y))


def send(value, way):
    return lax.ppermute(value, AXES, way)


def other(value):
    return send(value, OTHER_CORE)


def after(value, *earlier):
    return lax.optimization_barrier((value, *earlier))[0]


def weigh(own_ref, other_ref, weights_ref, out_ref):
    half = own_ref.shape[-1] // 2
    k = pl.program_id(0)
    away, y = lax.div(k, jnp.int32(Y)), rem(k, Y)
    side = rem(lax.div(lax.axis_index("col"), jnp.int32(Y)) + away, ZL)
    weights = weights_ref[side * Y + y]

    def put(panel_ref):
        panel = panel_ref[...].astype(jnp.float32)
        out_ref[:, :half] = (panel[:, half:] * weights).astype(jnp.bfloat16)
        out_ref[:, half:] = (panel[:, :half] * weights).astype(jnp.bfloat16)

    pl.when(away == 0)(lambda: put(own_ref))
    pl.when(away == 1)(lambda: put(other_ref))


def left_panel_of(own, others, weights):
    side, height, width = own.shape
    parts = ZL * side
    return pl.pallas_call(
        weigh,
        grid=(parts,),
        in_specs=[
            pl.BlockSpec((None, height, width), lambda k: (jnp.minimum(k, side - 1), 0, 0)),
            pl.BlockSpec((None, height, width), lambda k: (jnp.maximum(k - side, 0), 0, 0)),
            pl.BlockSpec((parts, 1, width // 2), lambda k: (0, 0, 0)),
        ],
        out_specs=pl.BlockSpec((None, height, width), lambda k: (k, 0, 0)),
        out_shape=jax.ShapeDtypeStruct((parts, height, width), jnp.bfloat16),
        compiler_params=pltpu.CompilerParams(vmem_limit_bytes=8 * 2**20),
        cost_estimate=pl.CostEstimate(flops=height, bytes_accessed=height * width, transcendentals=0),
        name="weigh_left",
    )(own, others, weights.reshape(parts, 1, width // 2))


def rem(value, length):
    return lax.rem(value, jnp.int32(length))


def join(left_ref, right_ref, out_ref, sems):
    half = left_ref.shape[-1]
    copies = [
        pltpu.make_async_copy(left_ref, out_ref.at[:, pl.ds(0, half)], sems.at[0]),
        pltpu.make_async_copy(right_ref, out_ref.at[:, pl.ds(half, half)], sems.at[1]),
    ]
    for copy in copies:
        copy.start()
    for copy in copies:
        copy.wait()


def side_by_side(first, second):
    height, width = first.shape
    anywhere = pl.BlockSpec(memory_space=pl.ANY)
    return pl.pallas_call(
        join,
        in_specs=[anywhere, anywhere],
        out_specs=anywhere,
        out_shape=jax.ShapeDtypeStruct((height, 2 * width), first.dtype),
        scratch_shapes=[pltpu.SemaphoreType.DMA((2,))],
        compiler_params=pltpu.CompilerParams(vmem_limit_bytes=4 * 2**20),
        name="join_shard",
    )(first, second)


def block_kernel(dz, places, operands, height, left_ref, *refs):
    arrays, gamma_ref = refs[:operands], refs[operands]
    out_ref, old, new, sems = refs[-4:]
    row, col = lax.axis_index("row"), lax.axis_index("col")
    zh, x, core = lax.div(row, jnp.int32(X * CORE)), rem(lax.div(row, jnp.int32(CORE)), X), rem(row, CORE)
    way = 2 * core - 1
    turn = rem(zh + dz[0] + dz[1] * way + 2 * ZH - lax.div(col, jnp.int32(2)), ZH)
    low, high = rem(turn, 2), lax.div(turn, jnp.int32(2))
    columns = pl.ds(pl.multiple_of((low * 2 + high) * height, 128), height)
    come = pltpu.make_async_copy(gamma_ref.at[:, columns], old, sems.at[0])
    come.start()
    left, right = [], []
    for array, skip, dx, other_core in places:
        zl, y = rem(core + other_core, CORE), rem(x + dx[0] + dx[1] * way + 2 * X - 2 * high, X)
        left.append(left_ref[rem(zl + lax.div(col, jnp.int32(Y)), ZL) * Y + y])
        right.append(arrays[array][skip * height : (skip + 1) * height, :])
    commutator = lax.dot_general(
        jnp.concatenate(left, 1),
        jnp.concatenate(right, 1),
        (((1,), (1,)), ((), ())),
        preferred_element_type=jnp.float32,
    )
    come.wait()
    new[...] = (old[...].astype(jnp.float32) + euler_step * commutator).astype(jnp.bfloat16)
    go = pltpu.make_async_copy(new, out_ref.at[:, columns], sems.at[1])
    go.start()
    go.wait()


def block_step(dz, pieces, left, gamma, out):
    arrays = []
    places = []
    for array, skip, dx, core in pieces:
        known = [index for index, had in enumerate(arrays) if had is array]
        if not known:
            known = [len(arrays)]
            arrays.append(array)
        places.append((known[0], skip, dx, core))
    height, count, width = left.shape[1], len(pieces), arrays[0].shape[-1]
    anywhere = pl.BlockSpec(memory_space=pl.ANY)
    operands = [left, *arrays, gamma]
    aliases = {}
    if out is not None:
        aliases = {len(operands): 0}
        operands.append(out)
    return pl.pallas_call(
        functools.partial(block_kernel, dz, places, len(arrays), height),
        in_specs=[
            *[pl.BlockSpec(memory_space=pltpu.VMEM)] * (1 + len(arrays)),
            *[anywhere] * (len(operands) - 1 - len(arrays)),
        ],
        out_specs=anywhere,
        out_shape=jax.ShapeDtypeStruct(gamma.shape, gamma.dtype),
        input_output_aliases=aliases,
        scratch_shapes=[
            pltpu.VMEM((height, height), jnp.bfloat16),
            pltpu.VMEM((height, height), jnp.bfloat16),
            pltpu.SemaphoreType.DMA((2,)),
        ],
        compiler_params=pltpu.CompilerParams(vmem_limit_bytes=20 * 2**20),
        cost_estimate=pl.CostEstimate(
            flops=height * height, bytes_accessed=height * height, transcendentals=0
        ),
        name="block_step",
    )(*operands)


HERE, BACK, AHEAD, ACROSS = (0, 0), (0, 1), (0, -1), (2, 0)


def per_device(eta_ladder, gamma_ladder, occupation, gamma):
    weights = 1.0 - 0.5 * occupation.astype(jnp.float32)
    shard = side_by_side(gamma_ladder, eta_ladder)
    height = shard.shape[0]
    alike_y = [[zl * Y + y for y in range(Y)] for zl in range(ZL)]
    own = lax.all_gather(shard, "col", axis_index_groups=alike_y)

    other_zl = send(shard, OTHER_ZL)
    p = after(send(shard, TO_HOME), other_zl)
    others = lax.all_gather(after(other_zl, p), "col", axis_index_groups=alike_y)
    ps = other(p)
    xp, xps = send(p, ALONG_X), send(ps, ALONG_X)
    zz = send(jnp.concatenate([p, ps], 0), ALONG_Z)
    fxp = send(after(xp, own), ALONG_X)
    their = [other(xp), other(xps), other(fxp)]
    zz = after(zz, xps, fxp)
    zs = other(zz)
    z2 = send(zz[:height], ALONG_Z)
    xzz, xzs = send(zz, ALONG_X), send(zs, ALONG_X)
    z2 = after(z2, xzz, *their)
    z2s = other(z2)
    fxzz = send(xzz, ALONG_X)
    xz2, xz2s = send(z2, ALONG_X), send(z2s, ALONG_X)

    left = left_panel_of(own, after(others, z2s), weights)

    def both(arrays, first_core):
        return [
            (array, half, dx, core)
            for array, dx in zip(arrays, (HERE, BACK, AHEAD, ACROSS))
            for half, core in ((0, first_core), (1, 1 - first_core))
        ]

    def alike(mine, swapped, x_mine, x_swapped, their_x, their_x_swapped, fx_mine, their_fx):
        return [
            (mine, 0, HERE, 0),
            (swapped, 0, HERE, 1),
            (x_mine, 0, BACK, 0),
            (x_swapped, 0, BACK, 1),
            (their_x, 0, AHEAD, 1),
            (their_x_swapped, 0, AHEAD, 0),
            (fx_mine, 0, ACROSS, 0),
            (their_fx, 0, ACROSS, 1),
        ]

    out = block_step(HERE, alike(p, ps, xp, xps, their[0], their[1], fxp, their[2]), left, gamma, None)
    their_fxzz = other(after(fxzz, out, xz2, xz2s))
    out = block_step(BACK, both([zz, xzz, other(xzs), fxzz], 0), left, gamma, out)
    fxz2 = send(after(xz2, out), ALONG_X)
    out = block_step(AHEAD, both([zs, xzs, other(xzz), their_fxzz], 1), left, gamma, out)
    their_fx = other(after(fxz2, out))
    return block_step(ACROSS, alike(z2, z2s, xz2, xz2s, other(xz2), other(xz2s), fxz2, their_fx), left, gamma, out)


def solution(mesh):
    placed = (P("row", "col"), P("row", "col"), P(), P("row", "col"))
    return jax.shard_map(
        per_device, mesh=mesh, in_specs=placed, out_specs=P("row", "col"), check_vma=False
    )
```

```python
import functools

import jax
import jax.numpy as jnp
from jax import lax
from jax.experimental import pallas as pl
from jax.experimental.pallas import tpu as pltpu
from jax.sharding import PartitionSpec as P

euler_step = 0.5
ZH, X, CORE, ZL, Y = 4, 4, 2, 2, 4
AXES = ("row", "col")


def every_device():
    for zh in range(ZH):
        for x in range(X):
            for core in range(CORE):
                for zl in range(ZL):
                    for y in range(Y):
                        yield zh, x, core, zl, y


def flat(zh, x, core, zl, y):
    return ((((zh % ZH) * X + x % X) * CORE + core % CORE) * ZL + zl % ZL) * Y + y % Y


def home(zh, x, core, zl, y):
    group = zh * 2 + x // 2
    return flat(zh + 2 * core + x % 2, y + 2 * core, zl, group // Y, group % Y)


def pairs(target):
    return [(flat(*d), target(*d)) for d in every_device()]


TO_HOME = pairs(home)
ALONG_Z = pairs(lambda zh, x, core, zl, y: flat(zh + 1 - 2 * core, x, core, zl, y))
ALONG_X = pairs(lambda zh, x, core, zl, y: flat(zh, x + 1 - 2 * core, core, zl, y))
OTHER_ZL = pairs(lambda zh, x, core, zl, y: flat(zh, x, core, zl + 1, y))
OTHER_CORE = pairs(lambda zh, x, core, zl, y: flat(zh, x, core + 1, zl, y))


def send(value, way):
    return lax.ppermute(value, AXES, way)


def other(value):
    return send(value, OTHER_CORE)


def after(value, *earlier):
    return lax.optimization_barrier((value, *earlier))[0]


def weigh(own_ref, other_ref, weights_ref, out_ref):
    half = own_ref.shape[-1] // 2
    k = pl.program_id(0)
    away, y = lax.div(k, jnp.int32(Y)), rem(k, Y)
    side = rem(lax.div(lax.axis_index("col"), jnp.int32(Y)) + away, ZL)
    weights = weights_ref[side * Y + y]

    def put(panel_ref):
        panel = panel_ref[...].astype(jnp.float32)
        out_ref[:, :half] = (panel[:, half:] * weights).astype(jnp.bfloat16)
        out_ref[:, half:] = (panel[:, :half] * weights).astype(jnp.bfloat16)

    pl.when(away == 0)(lambda: put(own_ref))
    pl.when(away == 1)(lambda: put(other_ref))


def left_panel_of(own, others, weights):
    side, height, width = own.shape
    parts = ZL * side
    return pl.pallas_call(
        weigh,
        grid=(parts,),
        in_specs=[
            pl.BlockSpec((None, height, width), lambda k: (jnp.minimum(k, side - 1), 0, 0)),
            pl.BlockSpec((None, height, width), lambda k: (jnp.maximum(k - side, 0), 0, 0)),
            pl.BlockSpec((parts, 1, width // 2), lambda k: (0, 0, 0)),
        ],
        out_specs=pl.BlockSpec((None, height, width), lambda k: (k, 0, 0)),
        out_shape=jax.ShapeDtypeStruct((parts, height, width), jnp.bfloat16),
        compiler_params=pltpu.CompilerParams(vmem_limit_bytes=8 * 2**20),
        cost_estimate=pl.CostEstimate(flops=height, bytes_accessed=height * width, transcendentals=0),
        name="weigh_left",
    )(own, others, weights.reshape(parts, 1, width // 2))


def rem(value, length):
    return lax.rem(value, jnp.int32(length))


def join(left_ref, right_ref, out_ref, sems):
    half = left_ref.shape[-1]
    copies = [
        pltpu.make_async_copy(left_ref, out_ref.at[:, pl.ds(0, half)], sems.at[0]),
        pltpu.make_async_copy(right_ref, out_ref.at[:, pl.ds(half, half)], sems.at[1]),
    ]
    for copy in copies:
        copy.start()
    for copy in copies:
        copy.wait()


def side_by_side(first, second):
    height, width = first.shape
    anywhere = pl.BlockSpec(memory_space=pl.ANY)
    return pl.pallas_call(
        join,
        in_specs=[anywhere, anywhere],
        out_specs=anywhere,
        out_shape=jax.ShapeDtypeStruct((height, 2 * width), first.dtype),
        scratch_shapes=[pltpu.SemaphoreType.DMA((2,))],
        compiler_params=pltpu.CompilerParams(vmem_limit_bytes=4 * 2**20),
        name="join_shard",
    )(first, second)


def block_kernel(dz, places, operands, height, left_ref, *refs):
    arrays, gamma_ref = refs[:operands], refs[operands]
    out_ref, old, new, sems = refs[-4:]
    row, col = lax.axis_index("row"), lax.axis_index("col")
    zh, x, core = lax.div(row, jnp.int32(X * CORE)), rem(lax.div(row, jnp.int32(CORE)), X), rem(row, CORE)
    way = 2 * core - 1
    turn = rem(zh + dz[0] + dz[1] * way + 2 * ZH - lax.div(col, jnp.int32(2)), ZH)
    low, high = rem(turn, 2), lax.div(turn, jnp.int32(2))
    columns = pl.ds(pl.multiple_of((low * 2 + high) * height, 128), height)
    come = pltpu.make_async_copy(gamma_ref.at[:, columns], old, sems.at[0])
    come.start()
    left, right = [], []
    for array, skip, dx, other_core in places:
        zl, y = rem(core + other_core, CORE), rem(x + dx[0] + dx[1] * way + 2 * X - 2 * high, X)
        left.append(left_ref[rem(zl + lax.div(col, jnp.int32(Y)), ZL) * Y + y])
        right.append(arrays[array][skip * height : (skip + 1) * height, :])
    commutator = lax.dot_general(
        jnp.concatenate(left, 1),
        jnp.concatenate(right, 1),
        (((1,), (1,)), ((), ())),
        preferred_element_type=jnp.float32,
    )
    come.wait()
    new[...] = (old[...].astype(jnp.float32) + euler_step * commutator).astype(jnp.bfloat16)
    go = pltpu.make_async_copy(new, out_ref.at[:, columns], sems.at[1])
    go.start()
    go.wait()


def block_step(dz, pieces, left, gamma, out):
    arrays = []
    places = []
    for array, skip, dx, core in pieces:
        known = [index for index, had in enumerate(arrays) if had is array]
        if not known:
            known = [len(arrays)]
            arrays.append(array)
        places.append((known[0], skip, dx, core))
    height, count, width = left.shape[1], len(pieces), arrays[0].shape[-1]
    anywhere = pl.BlockSpec(memory_space=pl.ANY)
    operands = [left, *arrays, gamma]
    aliases = {}
    if out is not None:
        aliases = {len(operands): 0}
        operands.append(out)
    return pl.pallas_call(
        functools.partial(block_kernel, dz, places, len(arrays), height),
        in_specs=[
            *[pl.BlockSpec(memory_space=pltpu.VMEM)] * (1 + len(arrays)),
            *[anywhere] * (len(operands) - 1 - len(arrays)),
        ],
        out_specs=anywhere,
        out_shape=jax.ShapeDtypeStruct(gamma.shape, gamma.dtype),
        input_output_aliases=aliases,
        scratch_shapes=[
            pltpu.VMEM((height, height), jnp.bfloat16),
            pltpu.VMEM((height, height), jnp.bfloat16),
            pltpu.SemaphoreType.DMA((2,)),
        ],
        compiler_params=pltpu.CompilerParams(vmem_limit_bytes=20 * 2**20),
        cost_estimate=pl.CostEstimate(
            flops=height * height, bytes_accessed=height * height, transcendentals=0
        ),
        name="block_step",
    )(*operands)


HERE, BACK, AHEAD, ACROSS = (0, 0), (0, 1), (0, -1), (2, 0)


def per_device(eta_ladder, gamma_ladder, occupation, gamma):
    weights = 1.0 - 0.5 * occupation.astype(jnp.float32)
    shard = side_by_side(gamma_ladder, eta_ladder)
    height = shard.shape[0]
    alike_y = [[zl * Y + y for y in range(Y)] for zl in range(ZL)]
    own = lax.all_gather(shard, "col", axis_index_groups=alike_y)

    other_zl = send(shard, OTHER_ZL)
    p = after(send(shard, TO_HOME), other_zl)
    others = lax.all_gather(after(other_zl, p), "col", axis_index_groups=alike_y)
    ps = other(p)
    xp, xps = send(p, ALONG_X), send(ps, ALONG_X)
    zz = send(jnp.concatenate([p, ps], 0), ALONG_Z)
    fxp = send(after(xp, own), ALONG_X)
    their = [other(xp), other(xps), other(fxp)]
    zz = after(zz, xps, fxp)
    zs = other(zz)
    z2 = send(zz[:height], ALONG_Z)
    xzz, xzs = send(zz, ALONG_X), send(zs, ALONG_X)
    z2 = after(z2, xzz, *their)
    z2s = other(z2)
    fxzz = send(xzz, ALONG_X)
    xz2, xz2s = send(z2, ALONG_X), send(z2s, ALONG_X)

    left = left_panel_of(own, after(others, z2s, xzs), weights)

    def both(arrays, first_core):
        return [
            (array, half, dx, core)
            for array, dx in zip(arrays, (HERE, BACK, AHEAD, ACROSS))
            for half, core in ((0, first_core), (1, 1 - first_core))
        ]

    def alike(mine, swapped, x_mine, x_swapped, their_x, their_x_swapped, fx_mine, their_fx):
        return [
            (mine, 0, HERE, 0),
            (swapped, 0, HERE, 1),
            (x_mine, 0, BACK, 0),
            (x_swapped, 0, BACK, 1),
            (their_x, 0, AHEAD, 1),
            (their_x_swapped, 0, AHEAD, 0),
            (fx_mine, 0, ACROSS, 0),
            (their_fx, 0, ACROSS, 1),
        ]

    out = block_step(HERE, alike(p, ps, xp, xps, their[0], their[1], fxp, their[2]), left, gamma, None)
    fxz2 = send(after(xz2, out), ALONG_X)
    their_fxzz = other(after(fxzz, out, xz2, xz2s))
    out = block_step(BACK, both([zz, xzz, other(xzs), fxzz], 0), left, gamma, out)
    out = block_step(AHEAD, both([zs, xzs, other(xzz), their_fxzz], 1), left, gamma, out)
    their_fx = other(after(fxz2, out))
    return block_step(ACROSS, alike(z2, z2s, xz2, xz2s, other(xz2), other(xz2s), fxz2, their_fx), left, gamma, out)


def solution(mesh):
    placed = (P("row", "col"), P("row", "col"), P(), P("row", "col"))
    return jax.shard_map(
        per_device, mesh=mesh, in_specs=placed, out_specs=P("row", "col"), check_vma=False
    )
```

```python
import functools

import jax
import jax.numpy as jnp
from jax import lax
from jax.experimental import pallas as pl
from jax.experimental.pallas import tpu as pltpu
from jax.sharding import PartitionSpec as P

euler_step = 0.5
ZH, X, CORE, ZL, Y = 4, 4, 2, 2, 4
AXES = ("row", "col")


def every_device():
    for zh in range(ZH):
        for x in range(X):
            for core in range(CORE):
                for zl in range(ZL):
                    for y in range(Y):
                        yield zh, x, core, zl, y


def flat(zh, x, core, zl, y):
    return ((((zh % ZH) * X + x % X) * CORE + core % CORE) * ZL + zl % ZL) * Y + y % Y


def home(zh, x, core, zl, y):
    group = zh * 2 + x // 2
    return flat(zh + 2 * core + x % 2, y + 2 * core, zl, group // Y, group % Y)


def pairs(target):
    return [(flat(*d), target(*d)) for d in every_device()]


TO_HOME = pairs(home)
ALONG_Z = pairs(lambda zh, x, core, zl, y: flat(zh + 1 - 2 * core, x, core, zl, y))
ALONG_X = pairs(lambda zh, x, core, zl, y: flat(zh, x + 1 - 2 * core, core, zl, y))
OTHER_ZL = pairs(lambda zh, x, core, zl, y: flat(zh, x, core, zl + 1, y))
OTHER_CORE = pairs(lambda zh, x, core, zl, y: flat(zh, x, core + 1, zl, y))


def send(value, way):
    return lax.ppermute(value, AXES, way)


def other(value):
    return send(value, OTHER_CORE)


def after(value, *earlier):
    return lax.optimization_barrier((value, *earlier))[0]


def weigh(away, panel_ref, weights_ref, *refs):
    out_ref = refs[-1]
    half = panel_ref.shape[-1] // 2
    side = rem(lax.div(lax.axis_index("col"), jnp.int32(Y)) + away, ZL)
    weights = weights_ref[side * Y + pl.program_id(0)]
    panel = panel_ref[...].astype(jnp.float32)
    out_ref[:, :half] = (panel[:, half:] * weights).astype(jnp.bfloat16)
    out_ref[:, half:] = (panel[:, :half] * weights).astype(jnp.bfloat16)


def left_panel_half(away, gathered, weights, out):
    side, height, width = gathered.shape
    parts = ZL * side
    operands = [gathered, weights.reshape(parts, 1, width // 2)]
    specs = [
        pl.BlockSpec((None, height, width), lambda k: (k, 0, 0)),
        pl.BlockSpec((parts, 1, width // 2), lambda k: (0, 0, 0)),
    ]
    if out is not None:
        operands.append(out)
        specs.append(pl.BlockSpec(memory_space=pl.ANY))
    return pl.pallas_call(
        functools.partial(weigh, away),
        grid=(side,),
        in_specs=specs,
        out_specs=pl.BlockSpec((None, height, width), lambda k: (k + away * side, 0, 0)),
        out_shape=jax.ShapeDtypeStruct((parts, height, width), jnp.bfloat16),
        input_output_aliases={} if out is None else {2: 0},
        compiler_params=pltpu.CompilerParams(vmem_limit_bytes=8 * 2**20),
        cost_estimate=pl.CostEstimate(flops=height, bytes_accessed=height * width, transcendentals=0),
        name="weigh_left",
    )(*operands)


def rem(value, length):
    return lax.rem(value, jnp.int32(length))


def join(left_ref, right_ref, out_ref, sems):
    half = left_ref.shape[-1]
    copies = [
        pltpu.make_async_copy(left_ref, out_ref.at[:, pl.ds(0, half)], sems.at[0]),
        pltpu.make_async_copy(right_ref, out_ref.at[:, pl.ds(half, half)], sems.at[1]),
    ]
    for copy in copies:
        copy.start()
    for copy in copies:
        copy.wait()


def side_by_side(first, second):
    height, width = first.shape
    anywhere = pl.BlockSpec(memory_space=pl.ANY)
    return pl.pallas_call(
        join,
        in_specs=[anywhere, anywhere],
        out_specs=anywhere,
        out_shape=jax.ShapeDtypeStruct((height, 2 * width), first.dtype),
        scratch_shapes=[pltpu.SemaphoreType.DMA((2,))],
        compiler_params=pltpu.CompilerParams(vmem_limit_bytes=4 * 2**20),
        name="join_shard",
    )(first, second)


def block_kernel(dz, places, operands, height, left_ref, *refs):
    arrays, gamma_ref = refs[:operands], refs[operands]
    out_ref, old, new, sems = refs[-4:]
    row, col = lax.axis_index("row"), lax.axis_index("col")
    zh, x, core = lax.div(row, jnp.int32(X * CORE)), rem(lax.div(row, jnp.int32(CORE)), X), rem(row, CORE)
    way = 2 * core - 1
    turn = rem(zh + dz[0] + dz[1] * way + 2 * ZH - lax.div(col, jnp.int32(2)), ZH)
    low, high = rem(turn, 2), lax.div(turn, jnp.int32(2))
    columns = pl.ds(pl.multiple_of((low * 2 + high) * height, 128), height)
    come = pltpu.make_async_copy(gamma_ref.at[:, columns], old, sems.at[0])
    come.start()
    left, right = [], []
    for array, skip, dx, other_core in places:
        zl, y = rem(core + other_core, CORE), rem(x + dx[0] + dx[1] * way + 2 * X - 2 * high, X)
        left.append(left_ref[rem(zl + lax.div(col, jnp.int32(Y)), ZL) * Y + y])
        right.append(arrays[array][skip * height : (skip + 1) * height, :])
    commutator = lax.dot_general(
        jnp.concatenate(left, 1),
        jnp.concatenate(right, 1),
        (((1,), (1,)), ((), ())),
        preferred_element_type=jnp.float32,
    )
    come.wait()
    new[...] = (old[...].astype(jnp.float32) + euler_step * commutator).astype(jnp.bfloat16)
    go = pltpu.make_async_copy(new, out_ref.at[:, columns], sems.at[1])
    go.start()
    go.wait()


def block_step(dz, pieces, left, gamma, out):
    arrays = []
    places = []
    for array, skip, dx, core in pieces:
        known = [index for index, had in enumerate(arrays) if had is array]
        if not known:
            known = [len(arrays)]
            arrays.append(array)
        places.append((known[0], skip, dx, core))
    height, count, width = left.shape[1], len(pieces), arrays[0].shape[-1]
    anywhere = pl.BlockSpec(memory_space=pl.ANY)
    operands = [left, *arrays, gamma]
    aliases = {}
    if out is not None:
        aliases = {len(operands): 0}
        operands.append(out)
    return pl.pallas_call(
        functools.partial(block_kernel, dz, places, len(arrays), height),
        in_specs=[
            *[pl.BlockSpec(memory_space=pltpu.VMEM)] * (1 + len(arrays)),
            *[anywhere] * (len(operands) - 1 - len(arrays)),
        ],
        out_specs=anywhere,
        out_shape=jax.ShapeDtypeStruct(gamma.shape, gamma.dtype),
        input_output_aliases=aliases,
        scratch_shapes=[
            pltpu.VMEM((height, height), jnp.bfloat16),
            pltpu.VMEM((height, height), jnp.bfloat16),
            pltpu.SemaphoreType.DMA((2,)),
        ],
        compiler_params=pltpu.CompilerParams(vmem_limit_bytes=20 * 2**20),
        cost_estimate=pl.CostEstimate(
            flops=height * height, bytes_accessed=height * height, transcendentals=0
        ),
        name="block_step",
    )(*operands)


HERE, BACK, AHEAD, ACROSS = (0, 0), (0, 1), (0, -1), (2, 0)


def per_device(eta_ladder, gamma_ladder, occupation, gamma):
    weights = 1.0 - 0.5 * occupation.astype(jnp.float32)
    shard = side_by_side(gamma_ladder, eta_ladder)
    height = shard.shape[0]
    alike_y = [[zl * Y + y for y in range(Y)] for zl in range(ZL)]
    own = lax.all_gather(shard, "col", axis_index_groups=alike_y)

    other_zl = send(shard, OTHER_ZL)
    p = after(send(shard, TO_HOME), other_zl)
    others = lax.all_gather(after(other_zl, p), "col", axis_index_groups=alike_y)
    ps = other(p)
    xp, xps = send(p, ALONG_X), send(ps, ALONG_X)
    zz = send(jnp.concatenate([p, ps], 0), ALONG_Z)
    fxp = send(after(xp, own), ALONG_X)
    their = [other(xp), other(xps), other(fxp)]
    zz = after(zz, xps, fxp)
    zs = other(zz)
    z2 = send(zz[:height], ALONG_Z)
    xzz, xzs = send(zz, ALONG_X), send(zs, ALONG_X)
    half_left = left_panel_half(0, own, weights, None)
    z2 = after(z2, xzz, half_left, *their)
    z2s = other(z2)
    fxzz = send(xzz, ALONG_X)
    xz2, xz2s = send(z2, ALONG_X), send(z2s, ALONG_X)

    left = left_panel_half(1, after(others, z2s, xzs), weights, half_left)

    def both(arrays, first_core):
        return [
            (array, half, dx, core)
            for array, dx in zip(arrays, (HERE, BACK, AHEAD, ACROSS))
            for half, core in ((0, first_core), (1, 1 - first_core))
        ]

    def alike(mine, swapped, x_mine, x_swapped, their_x, their_x_swapped, fx_mine, their_fx):
        return [
            (mine, 0, HERE, 0),
            (swapped, 0, HERE, 1),
            (x_mine, 0, BACK, 0),
            (x_swapped, 0, BACK, 1),
            (their_x, 0, AHEAD, 1),
            (their_x_swapped, 0, AHEAD, 0),
            (fx_mine, 0, ACROSS, 0),
            (their_fx, 0, ACROSS, 1),
        ]

    out = block_step(HERE, alike(p, ps, xp, xps, their[0], their[1], fxp, their[2]), left, gamma, None)
    fxz2 = send(after(xz2, out), ALONG_X)
    their_fxzz = other(after(fxzz, out, xz2))
    out = block_step(BACK, both([zz, xzz, other(xzs), fxzz], 0), left, gamma, out)
    their_xz2s = other(after(xz2s, out))
    out = block_step(AHEAD, both([zs, xzs, other(xzz), their_fxzz], 1), left, gamma, out)
    their_fx = other(after(fxz2, out))
    return block_step(ACROSS, alike(z2, z2s, xz2, xz2s, other(xz2), their_xz2s, fxz2, their_fx), left, gamma, out)


def solution(mesh):
    placed = (P("row", "col"), P("row", "col"), P(), P("row", "col"))
    return jax.shard_map(
        per_device, mesh=mesh, in_specs=placed, out_specs=P("row", "col"), check_vma=False
    )
```
